32 devices in a mesh: seq: 8 (over z, y), head: 4 (over x, core).
Axes of the slice: x: 2, y: 2, z: 4, core: 2. Of those that a mesh axis runs over, the one named last changes fastest.
Arguments:
- mixer_queries: bfloat16 [4096, 2048], P('seq', 'head'), may hold values from -6 to 6
- mixer_keys: bfloat16 [4096, 2048], P('seq', 'head'), may hold values from -6 to 6
- mixer_values: bfloat16 [4096, 2048], P('seq', 'head'), may hold values from -6 to 6
- window_keys: bfloat16 [4096, 512], P('seq', 'head'), may hold values from -1800 to 1800
- window_values: bfloat16 [4096, 512], P('seq', 'head'), may hold values from -6 to 6
- out_gain: float32 [2048], P('head'), may hold values from 0.1 to 1.9
- ridge: float32 [16], P('head'), may hold values from 0.25 to 4
- out_weight: bfloat16 [2048, 2048], P('head'), may hold values from -0.125 to 0.125
Outputs:
- layer_output: bfloat16 [4096, 2048], P('seq', 'head')
The draws below stay inside these ranges and needn't reach their ends.
All inputs are finite; a program needn't handle non-finite values.
Results may differ from the reference program's by a relative error of at most 0.019.
Values may be sent and summed in bfloat16 or wider, within the bound.
No kernel may reach another device: no remote copies, remote signals or barrier semaphores. Data moves between devices by JAX's collectives and lax.ppermute only.
A program may use at most 128 MiB of HBM per device.

```python
import math
import jax
import jax.numpy as jnp
from jax import lax

HEAD_DIM = 128
HEADS = 16
KV_HEADS = 4
D = 2048
SPAN = 128
ITERS = 8
WINDOW = 512
TOKENS = 4096


def draw_window_keys(key, part):
    key = jax.random.fold_in(key, 7)
    first_key = jax.random.fold_in(key, 0)
    values_out = jnp.clip(jax.random.normal(first_key, (TOKENS, KV_HEADS * HEAD_DIM), jnp.float32), -6.0, 6.0)
    return values_out.astype(jnp.bfloat16)


def levels(key, dims, pieces, least, high):
    loudness, own = 1.0, jax.random.fold_in(key, 6)
    for position, shards_of in pieces:
        heights = jnp.exp(jax.random.uniform(jax.random.fold_in(own, position), (shards_of,), jnp.float32, least / len(pieces), high / len(pieces)))
        loudness = loudness * jnp.repeat(heights, dims[position] // shards_of).reshape([-1 if axis == position else 1 for axis in range(len(dims))])
    return loudness


def noise(stream_key, extent, spread, reach, shards=(), kind=jnp.bfloat16):
    array = spread * jax.random.normal(stream_key, extent, jnp.float32)
    if shards:
        array = array * levels(stream_key, extent, shards, -0.22, 0.18)
    return jnp.clip(array, -reach, reach).astype(kind)


def setup_inputs(seed: int = 0) -> dict:
    streams_of = jax.random.split(jax.random.key(seed), 9)
    mixer_queries = noise(streams_of[0], (TOKENS, HEADS * HEAD_DIM), 1.0, 6.0, ((0, 8), (1, 4)))
    mixer_keys = noise(streams_of[1], (TOKENS, HEADS * HEAD_DIM), 1.0, 6.0, ((0, 8), (1, 4)))
    mixer_values = noise(streams_of[2], (TOKENS, HEADS * HEAD_DIM), 1.0, 6.0, ((0, 8), (1, 4)))
    window_keys = draw_window_keys(jax.random.fold_in(streams_of[8], 71), 0)
    window_values = noise(streams_of[4], (TOKENS, KV_HEADS * HEAD_DIM), 1.0, 6.0, ((0, 8), (1, 4)))
    out_gain = jnp.clip(1.0 + 0.18 * jax.random.normal(streams_of[5], (HEADS * HEAD_DIM,), jnp.float32), 0.1, 1.9)
    ridge = jnp.clip(jnp.exp(math.log(4.0) - 2.7725887 * jax.random.uniform(streams_of[6], (HEADS,), jnp.float32) ** levels(streams_of[6], (HEADS,), ((0, 4),), -0.2, 0.2)), 0.25, 4.0)
    out_weight = noise(streams_of[7], (HEADS * HEAD_DIM, D), (HEADS * HEAD_DIM) ** -0.5, 0.125, ((0, 4),))
    return dict(mixer_queries=mixer_queries, mixer_keys=mixer_keys, mixer_values=mixer_values, window_keys=window_keys, window_values=window_values, out_gain=out_gain, ridge=ridge, out_weight=out_weight)


HIGH = lax.Precision.HIGHEST
EPS = 1e-06

def unit_rows(block_in):
    row_width = block_in.shape[-1]
    return block_in * lax.rsqrt(lax.optimization_barrier(jnp.mean(block_in * block_in, axis=-1, keepdims=True)) + EPS) / math.sqrt(row_width)

def apply_state(states, keys_in, row_vals, vectors, lower_mask):
    inter = jnp.einsum('hcij,hclj->hcli', states, vectors, precision=HIGH)
    intersection = jnp.einsum('hcsj,hctj->hcts', keys_in, vectors, precision=HIGH) * lower_mask
    return inter + jnp.einsum('hcts,hcsi->hcti', intersection, row_vals, precision=HIGH)

def chebyshev(queries, keys_in, starts, ridge_col, upper, lower_mask, n_iters):
    centre = (upper + ridge_col) * 0.5
    radius = (upper - ridge_col) * 0.5
    solved = jnp.zeros_like(queries)
    residue = queries
    direction = residue
    step_size = 1.0 / centre
    for step_index in range(n_iters):
        if step_index > 0:
            scaled = radius * step_size
            weight_prev = scaled * scaled * (0.5 if step_index == 1 else 0.25)
            step_size = 1.0 / (centre - weight_prev / step_size)
            direction = residue + weight_prev * direction
        solved = solved + step_size * direction
        if step_index + 1 < n_iters:
            image_vec = apply_state(starts, keys_in, keys_in, direction, lower_mask) + ridge_col * direction
            residue = residue - step_size * image_vec
    return solved

def attend(q_part, k_part, v_part, row_first, col_first):
    scale = 1.0 / math.sqrt(q_part.shape[-1])
    scores = jnp.einsum('qkgd,skd->kgqs', q_part.astype(jnp.float32), k_part.astype(jnp.float32)) * scale
    rows_at = row_first + jnp.arange(q_part.shape[0], dtype=jnp.int32)
    cols_at = col_first + jnp.arange(k_part.shape[0], dtype=jnp.int32)
    allowed = (cols_at[None, :] >= 0) & (cols_at[None, :] <= rows_at[:, None]) & (cols_at[None, :] > rows_at[:, None] - WINDOW)
    scores = jnp.where(allowed[None, None], scores, -jnp.inf)
    peak = lax.optimization_barrier(jnp.max(scores, axis=-1, keepdims=True))
    expd = jnp.exp(scores - peak)
    weights = (expd / lax.optimization_barrier(jnp.sum(expd, axis=-1, keepdims=True))).astype(jnp.bfloat16)
    mixed_out = jnp.einsum('kgqs,skd->qkgd', weights.astype(jnp.float32), v_part.astype(jnp.float32))
    return mixed_out.astype(jnp.bfloat16).reshape(q_part.shape[0], -1)

def reference(mixer_queries, mixer_keys, mixer_values, window_keys, window_values, out_gain, ridge, out_weight):
    n_spans = TOKENS // SPAN
    lower_mask = (jnp.arange(SPAN)[:, None] >= jnp.arange(SPAN)[None, :]).astype(jnp.float32)
    ridge_col = ridge.astype(jnp.float32).reshape(HEADS, 1, 1, 1)
    gain_col = out_gain.astype(jnp.float32).reshape(HEADS, 1, 1, HEAD_DIM)

    def to_heads(rows_in):
        return rows_in.astype(jnp.float32).reshape(SPAN, HEADS, HEAD_DIM).transpose(1, 0, 2)[:, None]

    def span_step(carry, inputs):
        key_state, value_state = carry
        span_index, q_rows, k_rows, v_rows = inputs
        queries = unit_rows(to_heads(q_rows))
        keys_in = unit_rows(to_heads(k_rows))
        values_in = to_heads(v_rows)
        places = (span_index * SPAN + jnp.arange(SPAN, dtype=jnp.int32) + 1).astype(jnp.float32)
        upper = ridge_col + places.reshape(1, 1, SPAN, 1)
        solved = chebyshev(queries, keys_in, key_state[:, None], ridge_col, upper, lower_mask, ITERS)
        mixed = apply_state(value_state[:, None], keys_in, values_in, solved, lower_mask)
        normed = mixed * lax.rsqrt(lax.optimization_barrier(jnp.mean(mixed * mixed, axis=-1, keepdims=True)) + EPS) * gain_col
        rows_out = normed[:, 0].transpose(1, 0, 2).reshape(SPAN, HEADS * HEAD_DIM).astype(jnp.bfloat16)
        key_state = key_state + jnp.einsum('hld,hle->hde', keys_in[:, 0], keys_in[:, 0], precision=HIGH)
        value_state = value_state + jnp.einsum('hli,hlj->hij', values_in[:, 0], keys_in[:, 0], precision=HIGH)
        return ((key_state, value_state), rows_out)
    zero_state = jnp.zeros((HEADS, HEAD_DIM, HEAD_DIM), jnp.float32)
    inputs = (jnp.arange(n_spans, dtype=jnp.int32), mixer_queries.reshape(n_spans, SPAN, HEADS * HEAD_DIM), mixer_keys.reshape(n_spans, SPAN, HEADS * HEAD_DIM), mixer_values.reshape(n_spans, SPAN, HEADS * HEAD_DIM))
    _, attn_rows = lax.scan(span_step, (zero_state, zero_state), inputs)
    attn_rows = attn_rows.reshape(TOKENS, KV_HEADS, HEADS // KV_HEADS, HEAD_DIM)
    pad_zero = jnp.zeros((WINDOW, KV_HEADS, HEAD_DIM), jnp.bfloat16)
    keys_pad = jnp.concatenate([pad_zero, window_keys.reshape(TOKENS, KV_HEADS, HEAD_DIM)], 0)
    vals_pad = jnp.concatenate([pad_zero, window_values.reshape(TOKENS, KV_HEADS, HEAD_DIM)], 0)
    q_block = math.gcd(TOKENS, 512)

    def one_block(block_index):
        begin = (block_index * q_block).astype(jnp.int32)
        q_part = lax.dynamic_slice_in_dim(attn_rows, begin, q_block, 0)
        k_part = lax.dynamic_slice_in_dim(keys_pad, begin, q_block + WINDOW, 0)
        v_part = lax.dynamic_slice_in_dim(vals_pad, begin, q_block + WINDOW, 0)
        return attend(q_part, k_part, v_part, begin, begin - WINDOW)
    attended = lax.map(one_block, jnp.arange(TOKENS // q_block, dtype=jnp.int32)).reshape(TOKENS, HEADS * HEAD_DIM)
    return jnp.dot(attended, out_weight, preferred_element_type=jnp.float32).astype(jnp.bfloat16)
```

```python
import functools
import math

import jax
import jax.numpy as jnp
from jax import lax
from jax.experimental import pallas as pl
from jax.experimental.pallas import tpu as pltpu
from jax.sharding import PartitionSpec as P

ITERS = 8
WINDOW = 512
EPS = 1e-06
HEAD = 128
HALF = HEAD // 2
CHUNK = 256
PACKED = HALF + 8
GROUPS = 2
FAR = -1e30
F32 = jnp.float32
BF16 = jnp.bfloat16


def dot(a, b):
    return jnp.dot(a, b, preferred_element_type=F32)


def split(x):
    high = x.astype(BF16)
    return high, (x - high.astype(F32)).astype(BF16)


def unit(x):
    x = x.astype(F32)
    return x * (lax.rsqrt(jnp.mean(x * x, axis=-1, keepdims=True) + EPS) * (1.0 / math.sqrt(HEAD)))


def iota(shape, dim):
    return lax.broadcasted_iota(jnp.int32, shape, dim)


def head_cols(h):
    return slice(h * HEAD, (h + 1) * HEAD)


def pack(m):
    top, low = m[:HALF], pltpu.roll(m[HALF:], HALF, 1)
    row, col = iota((HALF, HEAD), 0), iota((HALF, HEAD), 1)
    body = jnp.where((col >= HALF) | (row > col), top, low)
    diag = jnp.sum(jnp.where(row == col, top, 0.0), axis=0, keepdims=True)
    return body, jnp.broadcast_to(diag, (8, HEAD))


def unpack(p):
    body, diag = p[:HALF], p[HALF : HALF + 1]
    row, col = iota((HALF, HEAD), 0), iota((HALF, HEAD), 1)
    top = jnp.where((col >= HALF) | (row > col), body, 0.0) + jnp.where(row == col, 0.5 * diag, 0.0)
    low = jnp.where((col < HALF) & (row <= col), body, 0.0) * jnp.where(row == col, 0.5, 1.0)
    half = jnp.concatenate([top, pltpu.roll(low, HALF, 1)], 0)
    return half + half.T


def moments_kernel(heads, keys_ref, out_ref):
    for h in range(heads):
        rows = unit(keys_ref[:, head_cols(h)])
        high, low = split(rows)
        high_t, low_t = split(rows.T)
        both = dot(high_t, jnp.concatenate([high, low], 1))
        body, diag = pack(both[:, :HEAD] + both[:, HEAD:] + dot(low_t, high))
        out_ref[h, :HALF] = body
        out_ref[h, HALF:] = diag


def prepare_kernel(
    heads, base_ref, ridge_ref, q_ref, k_ref, v_ref,
    total_ref, lk_ref, lkt_ref, qt_ref, vt_ref, kst_ref, vst_ref, coef_ref,
):
    rows = q_ref.shape[0]
    chunks = rows // CHUNK
    for h in range(heads):
        cols = head_cols(h)
        keys = unit(k_ref[:, cols])
        high, low = split(keys)
        high_t, low_t = split(keys.T)
        both = jnp.concatenate([high, low], 1)
        vals_t = v_ref[:, cols].astype(F32).T.astype(BF16)
        vt_ref[h] = vals_t
        qt_ref[h] = unit(q_ref[:, cols]).T
        key_sum = val_sum = None
        for c in range(chunks):
            span = slice(c * CHUNK, (c + 1) * CHUNK)
            if c:
                kst_ref[h, c - 1] = key_sum
                vst_ref[h, c - 1] = val_sum
            lk_ref[h, c, :CHUNK] = jnp.concatenate([high[span], high[span]], 1)
            lk_ref[h, c, CHUNK:] = jnp.concatenate([low[span], low[span]], 1)
            lkt_ref[h, c, :HEAD] = high_t[:, span]
            lkt_ref[h, c, HEAD:] = low_t[:, span]
            mv = dot(vals_t[:, span], both[span])
            mv = mv[:, :HEAD] + mv[:, HEAD:]
            val_sum = mv if c == 0 else val_sum + mv
            if c + 1 < chunks:
                mk = dot(high_t[:, span], both[span])
                mk = mk[:, :HEAD] + mk[:, HEAD:] + dot(low_t[:, span], high[span])
                key_sum = mk if c == 0 else key_sum + mk
        total_ref[h] = val_sum
        ridge = ridge_ref[h]
        places = (iota((1, rows), 1) + (base_ref[0] + 1)).astype(F32)
        upper = ridge + places
        centre = (upper + ridge) * 0.5
        radius = (upper - ridge) * 0.5
        step = 1.0 / centre
        weight = jnp.zeros_like(step)
        for i in range(ITERS):
            if i:
                scaled = radius * step
                weight = scaled * scaled * (0.5 if i == 1 else 0.25)
                step = 1.0 / (centre - weight / step)
            coef_ref[h, i : i + 1] = step
            coef_ref[h, ITERS + i : ITERS + i + 1] = weight


def gathered(flags_ref, part_refs, h):
    total = None
    for i, ref in enumerate(part_refs):
        part = jnp.where(flags_ref[i] > 0, ref[h], 0.0)
        total = part if total is None else total + part
    return total


def stack_state(state):
    high, low = split(state)
    return jnp.concatenate(
        [jnp.concatenate([high, high], 1), jnp.concatenate([low, low], 1)], 0
    )


def chebyshev_kernel(heads, parts, flags_ref, ridge_ref, *refs):
    part_refs, refs = refs[:parts], refs[parts:]
    qt_ref, lk_ref, lkt_ref, kst_ref, coef_ref, solved_ref, state, res, direction = refs
    chunks = lk_ref.shape[1]
    for h in range(heads):
        prior = unpack(gathered(flags_ref, part_refs, h))
        for c in range(chunks):
            state[h, c] = stack_state(prior if c == 0 else prior + kst_ref[h, c - 1])
        res[h] = qt_ref[h]
        direction[h] = jnp.zeros_like(direction[h])
        solved_ref[h] = jnp.zeros_like(solved_ref[h])
    keep = iota((CHUNK, CHUNK), 0) <= iota((CHUNK, CHUNK), 1)

    def advance(i, h, span):
        step = coef_ref[h, pl.ds(i, 1), span]
        weight = coef_ref[h, pl.ds(ITERS + i, 1), span]
        residue = res[h, :, span]
        way = residue + weight * direction[h, :, span]
        solved_ref[h, :, span] = solved_ref[h, :, span] + step * way
        return step, residue, way

    def body(i, carry):
        for h in range(heads):
            ridge = ridge_ref[h]
            for c in range(chunks):
                span = slice(c * CHUNK, (c + 1) * CHUNK)
                step, residue, way = advance(i, h, span)
                direction[h, :, span] = way
                right = jnp.concatenate(split(way), 0)
                inner = dot(lk_ref[h, c], right)
                inner = jnp.where(keep, inner[:CHUNK] + inner[CHUNK:], 0.0)
                high, low = split(inner)
                image = dot(state[h, c], right) + dot(lkt_ref[h, c], high)
                image = image[:HEAD] + image[HEAD:] + dot(lkt_ref[h, c, :HEAD], low)
                res[h, :, span] = residue - step * (image + ridge * way)
        return carry

    lax.fori_loop(0, ITERS - 1, body, 0)
    for h in range(heads):
        for c in range(chunks):
            advance(ITERS - 1, h, slice(c * CHUNK, (c + 1) * CHUNK))


def attend_kernel(heads, parts, first, flags_ref, base_ref, *refs):
    part_refs, refs = refs[:parts], refs[parts:]
    solved_ref, lk_ref, vt_ref, vst_ref, gain_ref, kp_ref, ko_ref, vp_ref, vo_ref, out_ref, kk, vv = refs
    chunks = lk_ref.shape[1]
    rows = ko_ref.shape[0]
    kk[:WINDOW] = kp_ref[...]
    kk[WINDOW:] = ko_ref[...]
    vv[:, :WINDOW] = vp_ref[...].astype(F32).T.astype(BF16)
    vv[:, WINDOW:] = vo_ref[...].astype(F32).T.astype(BF16)
    keep = iota((CHUNK, CHUNK), 0) <= iota((CHUNK, CHUNK), 1)
    bias = jnp.where(base_ref[0] > 0, 0.0, FAR).astype(F32)
    key_at, query_at = iota((HEAD, HEAD), 0), iota((HEAD, HEAD), 1)
    tiles = WINDOW // HEAD
    scale = 1.0 / math.sqrt(HEAD)
    for h in range(heads):
        prior = gathered(flags_ref, part_refs, h)
        gain = jnp.broadcast_to(gain_ref[:, head_cols(first + h)], (HEAD, HEAD)).T
        for c in range(chunks):
            span = slice(c * CHUNK, (c + 1) * CHUNK)
            right = jnp.concatenate(split(solved_ref[h, :, span]), 0)
            inner = dot(lk_ref[h, c], right)
            high, low = split(jnp.where(keep, inner[:CHUNK] + inner[CHUNK:], 0.0))
            mixed = dot(stack_state(prior if c == 0 else prior + vst_ref[h, c - 1]), right)
            vals = vt_ref[h, :, span]
            mixed = mixed[:HEAD] + mixed[HEAD:] + dot(vals, high) + dot(vals, low)
            rate = lax.rsqrt(jnp.mean(mixed * mixed, axis=0, keepdims=True) + EPS)
            for b in range(CHUNK // HEAD):
                lanes = slice(b * HEAD, (b + 1) * HEAD)
                query = (mixed[:, lanes] * rate[:, lanes] * gain).astype(BF16)
                j = c * (CHUNK // HEAD) + b
                near = slice(j * HEAD, (j + tiles + 1) * HEAD)
                scores = dot(kk[near], query)
                pieces = []
                for t in range(tiles + 1):
                    piece = scores[t * HEAD : (t + 1) * HEAD]
                    if t == 0:
                        piece = jnp.where(key_at > query_at, piece, FAR)
                    if t == tiles:
                        piece = jnp.where(key_at <= query_at, piece, FAR)
                    if j + t < tiles:
                        piece = piece + bias
                    pieces.append(piece)
                scores = jnp.concatenate(pieces, 0)
                peak = jnp.max(scores, axis=0, keepdims=True)
                grown = jnp.exp((scores - peak) * scale)
                share = 1.0 / jnp.sum(grown, axis=0, keepdims=True)
                weights = (grown * share).astype(BF16)
                mixed_vals = dot(vv[:, near], weights)
                out_ref[j * HEAD : (j + 1) * HEAD, head_cols(h)] = mixed_vals.T.astype(BF16)


def project_kernel(count, *refs):
    out_ref = refs[-1]
    total = None
    for i in range(count):
        part = dot(refs[i][...], refs[count + i][...])
        total = part if total is None else total + part
    out_ref[...] = total.astype(BF16)


SMEM = pl.BlockSpec(memory_space=pltpu.SMEM)
VMEM = pl.BlockSpec(memory_space=pltpu.VMEM)


def call(kernel, outs, args, scalars=0, scratch=(), flops=0, nbytes=0):
    return pl.pallas_call(
        kernel,
        out_shape=outs,
        in_specs=[SMEM] * scalars + [VMEM] * (len(args) - scalars),
        out_specs=jax.tree.map(lambda _: VMEM, outs),
        scratch_shapes=list(scratch),
        compiler_params=pltpu.CompilerParams(vmem_limit_bytes=40 * 1024 * 1024),
        cost_estimate=pl.CostEstimate(flops=flops, bytes_accessed=nbytes, transcendentals=0),
    )(*args)


def rounds_of(count):
    stride, rounds = 1, []
    while stride < count:
        left = count // stride
        radix = 4 if left % 4 == 0 else 2 if left % 2 == 0 else left
        rounds.append((stride, radix))
        stride *= radix
    return rounds


def partner(i, stride, radix, k):
    digit = (i // stride) % radix
    other = digit ^ k if radix in (2, 4) else (digit + k) % radix
    return i + (other - digit) * stride


def swap(x, axis, stride, radix, k):
    n = lax.axis_size(axis)
    return lax.ppermute(x, axis, [(i, partner(i, stride, radix, k)) for i in range(n)])


def source_digit(mine, stride, radix, k):
    digit = (mine // stride) % radix
    return digit ^ k if radix in (2, 4) else (digit - k) % radix


def before(value, axis):
    mine = lax.axis_index(axis)
    parts = []
    rounds = rounds_of(lax.axis_size(axis))
    for at, (stride, radix) in enumerate(rounds):
        got = [swap(value, axis, stride, radix, k) for k in range(1, radix)]
        parts += got
        if at + 1 < len(rounds):
            value = functools.reduce(jnp.add, got, value)
    return parts


def before_flags(axis):
    mine = lax.axis_index(axis)
    flags = []
    for stride, radix in rounds_of(lax.axis_size(axis)):
        digit = (mine // stride) % radix
        flags += [source_digit(mine, stride, radix, k) < digit for k in range(1, radix)]
    return jnp.stack(flags).astype(jnp.int32)


def shards(
    mixer_queries, mixer_keys, mixer_values, window_keys, window_values, out_gain, ridge, out_weight
):
    rows = mixer_queries.shape[0]
    heads = ridge.shape[0]
    chunks = rows // CHUNK
    seq, head = lax.axis_size("seq"), lax.axis_size("head")
    base = (lax.axis_index("seq") * rows).astype(jnp.int32).reshape(1)
    flags = before_flags("seq")
    per = heads // GROUPS
    shape = jax.ShapeDtypeStruct

    totals = call(
        functools.partial(moments_kernel, heads), shape((heads, PACKED, HEAD), F32), (mixer_keys,)
    )
    key_parts = before(totals, "seq")

    prepared = call(
        functools.partial(prepare_kernel, heads),
        (
            shape((heads, HEAD, HEAD), F32),
            shape((heads, chunks, 2 * CHUNK, 2 * HEAD), BF16),
            shape((heads, chunks, 2 * HEAD, CHUNK), BF16),
            shape((heads, HEAD, rows), F32),
            shape((heads, HEAD, rows), BF16),
            shape((heads, chunks - 1, HEAD, HEAD), F32),
            shape((heads, chunks - 1, HEAD, HEAD), F32),
            shape((heads, 2 * ITERS, rows), F32),
        ),
        (base, ridge, mixer_queries, mixer_keys, mixer_values),
        scalars=2,
    )
    val_total, lk, lkt, qt, vt, kst, vst, coef = prepared
    val_parts = before(val_total, "seq")
    rim = lax.ppermute(
        jnp.concatenate([window_keys, window_values], 1)[rows - WINDOW :],
        "seq",
        [(i, (i + 1) % seq) for i in range(seq)],
    )
    width = window_keys.shape[1]
    kp, vp = rim[:, :width], rim[:, width:]

    mine = lax.axis_index("head")
    cols = out_weight.shape[1] // head
    weights = []
    for k in range(head):
        other = partner(mine, 1, head, k) if head not in (2, 4) else mine ^ k
        piece = lax.dynamic_slice_in_dim(out_weight, other * cols, cols, 1)
        weights.append(piece if k == 0 else swap(piece, "head", 1, head, k))

    lefts, rights = [], []
    for g in range(GROUPS):
        part = slice(g * per, (g + 1) * per)
        solved = call(
            functools.partial(chebyshev_kernel, per, len(key_parts)),
            shape((per, HEAD, rows), F32),
            (flags, ridge[part], *[p[part] for p in key_parts], qt[part], lk[part], lkt[part], kst[part], coef[part]),
            scalars=2,
            scratch=(
                pltpu.VMEM((per, chunks, 2 * HEAD, 2 * HEAD), BF16),
                pltpu.VMEM((per, HEAD, rows), F32),
                pltpu.VMEM((per, HEAD, rows), F32),
            ),
            flops=10**10,
        )
        attended = call(
            functools.partial(attend_kernel, per, len(val_parts), g * per),
            shape((rows, per * HEAD), BF16),
            (
                flags, base, *[p[part] for p in val_parts], solved, lk[part], vt[part], vst[part],
                out_gain.reshape(1, -1), kp, window_keys, vp, window_values,
            ),
            scalars=2,
            scratch=(pltpu.VMEM((WINDOW + rows, width), BF16), pltpu.VMEM((width, WINDOW + rows), BF16)),
            flops=4 * 10**9,
        )
        span = slice(g * per * HEAD, (g + 1) * per * HEAD)
        if head == 4:
            far = swap(attended, "head", 1, 4, 2)
            got = [attended, swap(attended, "head", 1, 4, 1), far, swap(far, "head", 1, 4, 1)]
        else:
            got = [attended] + [swap(attended, "head", 1, head, k) for k in range(1, head)]
        lefts += got
        rights += [w[span] for w in weights]
    return call(
        functools.partial(project_kernel, len(lefts)), shape((rows, cols), BF16), (*lefts, *rights)
    )


def solution(mesh):
    return jax.shard_map(
        shards,
        mesh=mesh,
        in_specs=(
            P("seq", "head"),
            P("seq", "head"),
            P("seq", "head"),
            P("seq", "head"),
            P("seq", "head"),
            P("head"),
            P("head"),
            P("head", None),
        ),
        out_specs=P("seq", "head"),
        check_vma=False,
    )
```

```python
import functools
import math

import jax
import jax.numpy as jnp
from jax import lax
from jax.experimental import pallas as pl
from jax.experimental.pallas import tpu as pltpu
from jax.sharding import PartitionSpec as P

ITERS = 8
WINDOW = 512
EPS = 1e-06
HEAD = 128
HALF = HEAD // 2
CHUNK = 256
PACKED = HALF + 8
GROUPS = 2
FAR = -1e30
F32 = jnp.float32
BF16 = jnp.bfloat16


def dot(a, b):
    return jnp.dot(a, b, preferred_element_type=F32)


def split(x):
    high = x.astype(BF16)
    return high, (x - high.astype(F32)).astype(BF16)


def rate(x):
    return lax.rsqrt(jnp.mean(x * x, axis=-1, keepdims=True) + EPS) * (1.0 / math.sqrt(HEAD))


def unit(x):
    x = x.astype(F32)
    return x * rate(x)


def iota(shape, dim):
    return lax.broadcasted_iota(jnp.int32, shape, dim)


def head_cols(h):
    return slice(h * HEAD, (h + 1) * HEAD)


def pack(m):
    top, low = m[:HALF], pltpu.roll(m[HALF:], HALF, 1)
    row, col = iota((HALF, HEAD), 0), iota((HALF, HEAD), 1)
    body = jnp.where((col >= HALF) | (row > col), top, low)
    diag = jnp.sum(jnp.where(row == col, top, 0.0), axis=0, keepdims=True)
    return body, jnp.broadcast_to(diag, (8, HEAD))


def unpack(p):
    body, diag = p[:HALF], p[HALF : HALF + 1]
    row, col = iota((HALF, HEAD), 0), iota((HALF, HEAD), 1)
    top = jnp.where((col >= HALF) | (row > col), body, 0.0) + jnp.where(row == col, 0.5 * diag, 0.0)
    low = jnp.where((col < HALF) & (row <= col), body, 0.0) * jnp.where(row == col, 0.5, 1.0)
    half = jnp.concatenate([top, pltpu.roll(low, HALF, 1)], 0)
    return half + half.T


def moments_kernel(heads, keys_ref, out_ref):
    for h in range(heads):
        rows = keys_ref[:, head_cols(h)].astype(F32)
        scale = rate(rows)
        both = dot(rows.T.astype(BF16), jnp.concatenate(split(rows * (scale * scale)), 1))
        body, diag = pack(both[:, :HEAD] + both[:, HEAD:])
        out_ref[h, :HALF] = body
        out_ref[h, HALF:] = diag


def prepare_kernel(
    heads, groups, base_ref, ridge_ref, q_ref, k_ref, v_ref, wk_ref, wv_ref, total_ref, rim_ref, *outs
):
    rows = q_ref.shape[0]
    chunks = rows // CHUNK
    per = heads // groups
    keep = iota((HEAD, HEAD), 0) <= iota((HEAD, HEAD), 1)
    rim_ref[:, : wk_ref.shape[1]] = wk_ref[rows - WINDOW :]
    rim_ref[:, wk_ref.shape[1] :] = wv_ref[rows - WINDOW :]
    for head in range(heads):
        g, h = divmod(head, per)
        kk_ref, kt_ref, qt_ref, vt_ref, kst_ref, vst_ref, coef_ref, rate_ref, causal_ref = outs[9 * g : 9 * g + 9]
        cols = head_cols(head)
        raw = k_ref[:, cols]
        keys = raw.astype(F32)
        scale = rate(keys)
        square = jnp.broadcast_to(scale * scale, keys.shape)
        rate_ref[h] = jnp.broadcast_to(scale, keys.shape)
        keys_t = keys.T.astype(BF16)
        once = jnp.concatenate(split(keys * scale), 1)
        twice = jnp.concatenate(split(keys * square), 1)
        vals_t = v_ref[:, cols].astype(F32).T.astype(BF16)
        vt_ref[h] = vals_t
        qt_ref[h] = unit(q_ref[:, cols]).T
        key_sum = val_sum = None
        for c in range(chunks):
            span = slice(c * CHUNK, (c + 1) * CHUNK)
            if c:
                kst_ref[h, c - 1] = key_sum
                vst_ref[h, c - 1] = val_sum
            kk_ref[h, c] = jnp.concatenate([raw[span], raw[span]], 1)
            for r in range(CHUNK // HEAD):
                at = slice(c * CHUNK + r * HEAD, c * CHUNK + (r + 1) * HEAD)
                kt_ref[h, c, :, 2 * r * HEAD : (2 * r + 2) * HEAD] = jnp.concatenate([keys_t[:, at]] * 2, 1)
                across = jnp.where(keep, square[at], 0.0)
                causal_ref[h, c, r] = across
                if r == 0:
                    causal_ref[h, c, 2] = square[at]
            mv = dot(vals_t[:, span], once[span])
            mv = mv[:, :HEAD] + mv[:, HEAD:]
            val_sum = mv if c == 0 else val_sum + mv
            if c + 1 < chunks:
                mk = dot(keys_t[:, span], twice[span])
                mk = mk[:, :HEAD] + mk[:, HEAD:]
                key_sum = mk if c == 0 else key_sum + mk
        total_ref[head] = val_sum
        ridge = ridge_ref[head]
        places = (iota((1, rows), 1) + (base_ref[0] + 1)).astype(F32)
        upper = ridge + places
        centre = (upper + ridge) * 0.5
        radius = (upper - ridge) * 0.5
        step = 1.0 / centre
        weight = jnp.zeros_like(step)
        for i in range(ITERS):
            if i:
                scaled = radius * step
                weight = scaled * scaled * (0.5 if i == 1 else 0.25)
                step = 1.0 / (centre - weight / step)
            coef_ref[h, i : i + 1] = step
            coef_ref[h, ITERS + i : ITERS + i + 1] = weight


def gathered(flags_ref, part_refs, h):
    total = None
    for i, ref in enumerate(part_refs):
        part = jnp.where(flags_ref[i] > 0, ref[h], 0.0)
        total = part if total is None else total + part
    return total


def stack_state(state):
    high, low = split(state)
    return jnp.concatenate(
        [jnp.concatenate([high, high], 1), jnp.concatenate([low, low], 1)], 0
    )


def cheb_scratch(per, chunks):
    return (
        pltpu.VMEM((per, chunks, 2 * HEAD, 2 * HEAD), BF16),
        pltpu.VMEM((per, HEAD, chunks * CHUNK), F32),
        pltpu.VMEM((per, HEAD, chunks * CHUNK), F32),
        pltpu.VMEM((per, chunks, 2 * HEAD, CHUNK), BF16),
        pltpu.VMEM((per, chunks, CHUNK, CHUNK + HEAD), BF16),
    )


def chebyshev_kernel(heads, parts, first, flags_ref, ridge_ref, *refs):
    part_refs, refs = refs[:parts], refs[parts:]
    qt_ref, kk_ref, kt_ref, kst_ref, coef_ref, causal_ref, solved_ref, state, res, direction, rights, inners = refs
    chunks = kk_ref.shape[1]
    for h in range(heads):
        prior = unpack(gathered(flags_ref, part_refs, first + h))
        for c in range(chunks):
            state[h, c] = stack_state(prior if c == 0 else prior + kst_ref[h, c - 1])
        res[h] = qt_ref[h]
        direction[h] = jnp.zeros_like(direction[h])
        solved_ref[h] = jnp.zeros_like(solved_ref[h])
    chains = [(h, c) for h in range(heads) for c in range(chunks)]

    def span_of(c):
        return slice(c * CHUNK, (c + 1) * CHUNK)

    def advance(i, h, c):
        span = span_of(c)
        step = coef_ref[h, pl.ds(i, 1), span]
        weight = coef_ref[h, pl.ds(ITERS + i, 1), span]
        way = res[h, :, span] + weight * direction[h, :, span]
        solved_ref[h, :, span] = solved_ref[h, :, span] + step * way
        return way

    def stage1(i, h, c):
        way = advance(i, h, c)
        direction[h, :, span_of(c)] = way
        high, low = split(way)
        rights[h, c, :HEAD] = high
        rights[h, c, HEAD:] = low

    def stage2(i, h, c):
        inner = dot(kk_ref[h, c], rights[h, c])
        for r, cc, k in ((0, 0, 0), (0, 1, 2), (1, 1, 1)):
            tile = inner[r * HEAD : (r + 1) * HEAD, cc * HEAD : (cc + 1) * HEAD]
            high, low = split(tile * causal_ref[h, c, k])
            lanes = slice((r + cc) * HEAD, (r + cc + 1) * HEAD)
            inners[h, c, :HEAD, lanes] = high
            inners[h, c, HEAD:, lanes] = low

    def stage3(i, h, c):
        image = dot(state[h, c], rights[h, c])
        image = image[:HEAD] + image[HEAD:] + dot(kt_ref[h, c, :, :CHUNK], inners[h, c, :, :CHUNK])
        late = dot(kt_ref[h, c, :, CHUNK:], inners[h, c, :, CHUNK:])
        step = coef_ref[h, pl.ds(i, 1), span_of(c)]
        for k in range(CHUNK // HEAD):
            lanes = slice(k * HEAD, (k + 1) * HEAD)
            span = slice(c * CHUNK + k * HEAD, c * CHUNK + (k + 1) * HEAD)
            part = image[:, lanes] + late if k else image[:, lanes]
            res[h, :, span] = res[h, :, span] - step[:, lanes] * (part + ridge_ref[first + h] * direction[h, :, span])

    def body(i, carry):
        for ch in chains:
            stage1(i, *ch)
        for ch in chains:
            stage2(i, *ch)
        for ch in chains:
            stage3(i, *ch)
        return carry

    lax.fori_loop(0, ITERS - 1, body, 0)
    for h, c in chains:
        advance(ITERS - 1, h, c)


def attend_kernel(heads, parts, first, flags_ref, base_ref, *refs):
    part_refs, refs = refs[:parts], refs[parts:]
    solved_ref, kk_ref, rate_ref, vt_ref, vst_ref, gain_ref, rim_ref, ko_ref, vo_ref, out_ref, kk, vv = refs
    chunks = kk_ref.shape[1]
    rows = ko_ref.shape[0]
    width = ko_ref.shape[1]
    kk[:WINDOW] = rim_ref[:, :width]
    kk[WINDOW:] = ko_ref[...]
    vv[:, :WINDOW] = rim_ref[:, width:].astype(F32).T.astype(BF16)
    vv[:, WINDOW:] = vo_ref[...].astype(F32).T.astype(BF16)
    keep = iota((CHUNK, CHUNK), 0) <= iota((CHUNK, CHUNK), 1)
    bias = jnp.where(base_ref[0] > 0, 0.0, FAR).astype(F32)
    key_at, query_at = iota((HEAD, HEAD), 0), iota((HEAD, HEAD), 1)
    tiles = WINDOW // HEAD
    scale = 1.0 / math.sqrt(HEAD)
    for h in range(heads):
        prior = gathered(flags_ref, part_refs, first + h)
        gain = jnp.broadcast_to(gain_ref[:, head_cols(first + h)], (HEAD, HEAD)).T
        for c in range(chunks):
            span = slice(c * CHUNK, (c + 1) * CHUNK)
            right = jnp.concatenate(split(solved_ref[h, :, span]), 0)
            inner = dot(kk_ref[h, c], right)
            by = rate_ref[h, span]
            high, low = split(jnp.where(keep, inner * jnp.concatenate([by, by], 1), 0.0))
            mixed = dot(stack_state(prior if c == 0 else prior + vst_ref[h, c - 1]), right)
            vals = vt_ref[h, :, span]
            mixed = mixed[:HEAD] + mixed[HEAD:] + dot(vals, high) + dot(vals, low)
            rate = lax.rsqrt(jnp.mean(mixed * mixed, axis=0, keepdims=True) + EPS)
            for b in range(CHUNK // HEAD):
                lanes = slice(b * HEAD, (b + 1) * HEAD)
                query = (mixed[:, lanes] * rate[:, lanes] * gain).astype(BF16)
                j = c * (CHUNK // HEAD) + b
                near = slice(j * HEAD, (j + tiles + 1) * HEAD)
                scores = dot(kk[near], query)
                pieces = []
                for t in range(tiles + 1):
                    piece = scores[t * HEAD : (t + 1) * HEAD]
                    if t == 0:
                        piece = jnp.where(key_at > query_at, piece, FAR)
                    if t == tiles:
                        piece = jnp.where(key_at <= query_at, piece, FAR)
                    if j + t < tiles:
                        piece = piece + bias
                    pieces.append(piece)
                scores = jnp.concatenate(pieces, 0)
                peak = jnp.max(scores, axis=0, keepdims=True)
                grown = jnp.exp((scores - peak) * scale)
                share = 1.0 / jnp.sum(grown, axis=0, keepdims=True)
                weights = (grown * share).astype(BF16)
                mixed_vals = dot(vv[:, near], weights)
                out_ref[j * HEAD : (j + 1) * HEAD, head_cols(h)] = mixed_vals.T.astype(BF16)


def project_kernel(groups, count, *refs):
    out_ref = refs[-1]
    total = None
    for g in range(groups):
        for i in range(count):
            left = refs[g * count + i]
            width = left.shape[1]
            part = dot(left[...], refs[groups * count + i][g * width : (g + 1) * width])
            total = part if total is None else total + part
    out_ref[...] = total.astype(BF16)


SMEM = pl.BlockSpec(memory_space=pltpu.SMEM)
VMEM = pl.BlockSpec(memory_space=pltpu.VMEM)


def call(kernel, outs, args, scalars=0, scratch=(), flops=0, nbytes=0):
    return pl.pallas_call(
        kernel,
        out_shape=outs,
        in_specs=[SMEM] * scalars + [VMEM] * (len(args) - scalars),
        out_specs=jax.tree.map(lambda _: VMEM, outs),
        scratch_shapes=list(scratch),
        compiler_params=pltpu.CompilerParams(vmem_limit_bytes=40 * 1024 * 1024),
        cost_estimate=pl.CostEstimate(flops=flops, bytes_accessed=nbytes, transcendentals=0),
    )(*args)


def rounds_of(count):
    stride, rounds = 1, []
    while stride < count:
        left = count // stride
        radix = 4 if left % 4 == 0 else 2 if left % 2 == 0 else left
        rounds.append((stride, radix))
        stride *= radix
    return rounds


def partner(i, stride, radix, k):
    digit = (i // stride) % radix
    other = digit ^ k if radix in (2, 4) else (digit + k) % radix
    return i + (other - digit) * stride


def swap(x, axis, stride, radix, k):
    n = lax.axis_size(axis)
    return lax.ppermute(x, axis, [(i, partner(i, stride, radix, k)) for i in range(n)])


def source_digit(mine, stride, radix, k):
    digit = (mine // stride) % radix
    return digit ^ k if radix in (2, 4) else (digit - k) % radix


def before(value, axis, at):
    rounds = rounds_of(lax.axis_size(axis))
    stride, radix = rounds[at]
    got = [swap(value, axis, stride, radix, k) for k in range(1, radix)]
    return got, functools.reduce(jnp.add, got, value) if at + 1 < len(rounds) else None


def before_flags(axis):
    mine = lax.axis_index(axis)
    flags = []
    for stride, radix in rounds_of(lax.axis_size(axis)):
        digit = (mine // stride) % radix
        flags += [source_digit(mine, stride, radix, k) < digit for k in range(1, radix)]
    return jnp.stack(flags).astype(jnp.int32)


def shards(
    mixer_queries, mixer_keys, mixer_values, window_keys, window_values, out_gain, ridge, out_weight
):
    rows = mixer_queries.shape[0]
    heads = ridge.shape[0]
    chunks = rows // CHUNK
    seq, head = lax.axis_size("seq"), lax.axis_size("head")
    base = (lax.axis_index("seq") * rows).astype(jnp.int32).reshape(1)
    flags = before_flags("seq")
    per = heads // GROUPS
    shape = jax.ShapeDtypeStruct

    key_total = call(
        functools.partial(moments_kernel, heads), shape((heads, PACKED, HEAD), F32), (mixer_keys,)
    )
    width = window_keys.shape[1]
    val_total, rim, *prepared = call(
        functools.partial(prepare_kernel, heads, GROUPS),
        (
            shape((heads, HEAD, HEAD), F32),
            shape((WINDOW, 2 * width), BF16),
            *GROUPS
            * (
                shape((per, chunks, CHUNK, 2 * HEAD), BF16),
                shape((per, chunks, HEAD, 2 * CHUNK), BF16),
                shape((per, HEAD, rows), F32),
                shape((per, HEAD, rows), BF16),
                shape((per, chunks - 1, HEAD, HEAD), F32),
                shape((per, chunks - 1, HEAD, HEAD), F32),
                shape((per, 2 * ITERS, rows), F32),
                shape((per, rows, HEAD), F32),
                shape((per, chunks, 3, HEAD, HEAD), F32),
            ),
        ),
        (base, ridge, mixer_queries, mixer_keys, mixer_values, window_keys, window_values),
        scalars=2,
    )
    key_parts, val_parts = [], []
    for at in range(len(rounds_of(seq))):
        got, following = before(key_total, "seq", at)
        key_parts += got
        if following is not None:
            key_total = following
            if at == 0:
                key_total, val_total, rim, out_weight = lax.optimization_barrier(
                    (key_total, val_total, rim, out_weight)
                )
    for at in range(len(rounds_of(seq))):
        got, following = before(val_total, "seq", at)
        val_parts += got
        if following is not None:
            val_total = following
            if at == 0:
                val_total, key_parts = lax.optimization_barrier((val_total, key_parts))
    rim = lax.ppermute(rim, "seq", [(i, (i + 1) % seq) for i in range(seq)])

    mine = lax.axis_index("head")
    cols = out_weight.shape[1] // head
    rights = []
    for k in range(head):
        piece = lax.dynamic_slice_in_dim(out_weight, partner(mine, 1, head, k) * cols, cols, 1)
        rights.append(piece if k == 0 else swap(piece, "head", 1, head, k))

    lefts = []
    for g in range(GROUPS):
        kk, kt, qt, vt, kst, vst, coef, rates, causal = prepared[9 * g : 9 * g + 9]
        solved = call(
            functools.partial(chebyshev_kernel, per, len(key_parts), g * per),
            shape((per, HEAD, rows), F32),
            (flags, ridge, *key_parts, qt, kk, kt, kst, coef, causal),
            scalars=2,
            scratch=cheb_scratch(per, chunks),
            flops=10**10,
            nbytes=3 * 10**7,
        )
        attended = call(
            functools.partial(attend_kernel, per, len(val_parts), g * per),
            shape((rows, per * HEAD), BF16),
            (
                flags, base, *val_parts, solved, kk, rates, vt, vst,
                out_gain.reshape(1, -1), rim, window_keys, window_values,
            ),
            scalars=2,
            scratch=(pltpu.VMEM((WINDOW + rows, width), BF16), pltpu.VMEM((width, WINDOW + rows), BF16)),
            flops=4 * 10**9,
            nbytes=15 * 10**6,
        )
        if head == 4:
            far = swap(attended, "head", 1, 4, 2)
            lefts += [attended, swap(attended, "head", 1, 4, 1), far, swap(far, "head", 1, 4, 1)]
        else:
            lefts += [attended] + [swap(attended, "head", 1, head, k) for k in range(1, head)]
    return call(
        functools.partial(project_kernel, GROUPS, head),
        shape((rows, cols), BF16),
        (*lefts, *rights),
    )


def solution(mesh):
    return jax.shard_map(
        shards,
        mesh=mesh,
        in_specs=(
            P("seq", "head"),
            P("seq", "head"),
            P("seq", "head"),
            P("seq", "head"),
            P("seq", "head"),
            P("head"),
            P("head"),
            P("head", None),
        ),
        out_specs=P("seq", "head"),
        check_vma=False,
    )
```

```python
import functools
import math

import jax
import jax.numpy as jnp
from jax import lax
from jax.experimental import pallas as pl
from jax.experimental.pallas import tpu as pltpu
from jax.sharding import PartitionSpec as P

ITERS = 8
WINDOW = 512
EPS = 1e-06
HEAD = 128
HALF = HEAD // 2
CHUNK = 256
PACKED = HALF + 8
BOTH = PACKED + HEAD
GROUPS = 2
FAR = -1e30
F32 = jnp.float32
BF16 = jnp.bfloat16


def dot(a, b):
    return jnp.dot(a, b, preferred_element_type=F32)


def split(x):
    high = x.astype(BF16)
    return high, (x - high.astype(F32)).astype(BF16)


def rate(x):
    return lax.rsqrt(jnp.mean(x * x, axis=-1, keepdims=True) + EPS) * (1.0 / math.sqrt(HEAD))


def unit(x):
    x = x.astype(F32)
    return x * rate(x)


def iota(shape, dim):
    return lax.broadcasted_iota(jnp.int32, shape, dim)


def head_cols(h):
    return slice(h * HEAD, (h + 1) * HEAD)


def pack(m):
    top, low = m[:HALF], pltpu.roll(m[HALF:], HALF, 1)
    row, col = iota((HALF, HEAD), 0), iota((HALF, HEAD), 1)
    body = jnp.where((col >= HALF) | (row > col), top, low)
    diag = jnp.sum(jnp.where(row == col, top, 0.0), axis=0, keepdims=True)
    return body, jnp.broadcast_to(diag, (8, HEAD))


def unpack(p):
    body, diag = p[:HALF], p[HALF : HALF + 1]
    row, col = iota((HALF, HEAD), 0), iota((HALF, HEAD), 1)
    top = jnp.where((col >= HALF) | (row > col), body, 0.0) + jnp.where(row == col, 0.5 * diag, 0.0)
    low = jnp.where((col < HALF) & (row <= col), body, 0.0) * jnp.where(row == col, 0.5, 1.0)
    half = jnp.concatenate([top, pltpu.roll(low, HALF, 1)], 0)
    return half + half.T


def moments_kernel(shares, digit_ref, keys_ref, vals_ref, *outs):
    own = outs[0].shape[0]
    for k in range(shares):
        for j in range(own):
            cols = pl.ds(pl.multiple_of(((digit_ref[0] ^ k) * own + j) * HEAD, HEAD), HEAD)
            keys = keys_ref[:, cols].astype(F32)
            scale = rate(keys)
            once = keys * scale
            pair = dot(keys.T.astype(BF16), jnp.concatenate(split(once * scale), 1))
            body, diag = pack(pair[:, :HEAD] + pair[:, HEAD:])
            outs[k][j, :HALF] = body
            outs[k][j, HALF:PACKED] = diag
            vals_t = vals_ref[:, cols].astype(F32).T.astype(BF16)
            pair = dot(vals_t, jnp.concatenate(split(once), 1))
            outs[k][j, PACKED:] = pair[:, :HEAD] + pair[:, HEAD:]


def prepare(heads, first, base_ref, ridge_ref, q_ref, k_ref, v_ref, *outs):
    rows = q_ref.shape[0]
    chunks = rows // CHUNK
    kk_ref, kt_ref, qt_ref, vt_ref, kst_ref, vst_ref, coef_ref, rate_ref, causal_ref = outs
    keep = iota((HEAD, HEAD), 0) <= iota((HEAD, HEAD), 1)
    for h in range(heads):
        cols = head_cols(first + h)
        raw = k_ref[:, cols]
        keys = raw.astype(F32)
        scale = rate(keys)
        square = jnp.broadcast_to(scale * scale, keys.shape)
        rate_ref[h] = jnp.broadcast_to(scale, keys.shape)
        keys_t = keys.T.astype(BF16)
        once = jnp.concatenate(split(keys * scale), 1)
        twice = jnp.concatenate(split(keys * square), 1)
        vals_t = v_ref[:, cols].astype(F32).T.astype(BF16)
        vt_ref[h] = vals_t
        qt_ref[h] = unit(q_ref[:, cols]).T
        key_sum = val_sum = None
        for c in range(chunks):
            span = slice(c * CHUNK, (c + 1) * CHUNK)
            if c:
                kst_ref[h, c - 1] = key_sum
                vst_ref[h, c - 1] = val_sum
            kk_ref[h, c] = jnp.concatenate([raw[span], raw[span]], 1)
            for r in range(CHUNK // HEAD):
                at = slice(c * CHUNK + r * HEAD, c * CHUNK + (r + 1) * HEAD)
                kt_ref[h, c, :, 2 * r * HEAD : (2 * r + 2) * HEAD] = jnp.concatenate([keys_t[:, at]] * 2, 1)
                across = jnp.where(keep, square[at], 0.0)
                causal_ref[h, c, r] = across
                if r == 0:
                    causal_ref[h, c, 2] = square[at]
            if c + 1 < chunks:
                mv = dot(vals_t[:, span], once[span])
                mv = mv[:, :HEAD] + mv[:, HEAD:]
                val_sum = mv if c == 0 else val_sum + mv
                mk = dot(keys_t[:, span], twice[span])
                mk = mk[:, :HEAD] + mk[:, HEAD:]
                key_sum = mk if c == 0 else key_sum + mk
        ridge = ridge_ref[first + h]
        places = (iota((1, rows), 1) + (base_ref[0] + 1)).astype(F32)
        upper = ridge + places
        centre = (upper + ridge) * 0.5
        radius = (upper - ridge) * 0.5
        step = 1.0 / centre
        weight = jnp.zeros_like(step)
        for i in range(ITERS):
            if i:
                scaled = radius * step
                weight = scaled * scaled * (0.5 if i == 1 else 0.25)
                step = 1.0 / (centre - weight / step)
            coef_ref[h, i : i + 1] = step
            coef_ref[h, ITERS + i : ITERS + i + 1] = weight


def gathered(digit_ref, part_refs, h, rows):
    own = part_refs[0].shape[0]
    total = None
    for k, ref in enumerate(part_refs):
        part = jnp.where((digit_ref[0] ^ k) == h // own, ref[h % own, rows], 0.0)
        total = part if total is None else total + part
    return total


def stack_state(state):
    high, low = split(state)
    return jnp.concatenate(
        [jnp.concatenate([high, high], 1), jnp.concatenate([low, low], 1)], 0
    )


def cheb_scratch(per, chunks):
    return (
        pltpu.VMEM((per, chunks, 2 * HEAD, 2 * HEAD), BF16),
        pltpu.VMEM((per, HEAD, chunks * CHUNK), F32),
        pltpu.VMEM((per, HEAD, chunks * CHUNK), F32),
        pltpu.VMEM((per, chunks, 2 * HEAD, CHUNK), BF16),
        pltpu.VMEM((per, chunks, CHUNK, CHUNK + HEAD), BF16),
    )


def chebyshev(heads, first, digit_ref, ridge_ref, part_refs, *refs):
    kk_ref, kt_ref, kst_ref, coef_ref, causal_ref, solved_ref, state, res, direction, rights, inners = refs
    chunks = kk_ref.shape[1]
    for h in range(heads):
        prior = unpack(gathered(digit_ref, part_refs, first + h, slice(0, PACKED)))
        for c in range(chunks):
            state[h, c] = stack_state(prior if c == 0 else prior + kst_ref[h, c - 1])
        direction[h] = jnp.zeros_like(direction[h])
        solved_ref[h] = jnp.zeros_like(solved_ref[h])
    chains = [(h, c) for h in range(heads) for c in range(chunks)]

    def span_of(c):
        return slice(c * CHUNK, (c + 1) * CHUNK)

    def advance(i, h, c):
        span = span_of(c)
        step = coef_ref[h, pl.ds(i, 1), span]
        weight = coef_ref[h, pl.ds(ITERS + i, 1), span]
        way = res[h, :, span] + weight * direction[h, :, span]
        solved_ref[h, :, span] = solved_ref[h, :, span] + step * way
        return way

    def stage1(i, h, c):
        way = advance(i, h, c)
        direction[h, :, span_of(c)] = way
        high, low = split(way)
        rights[h, c, :HEAD] = high
        rights[h, c, HEAD:] = low

    def stage2(i, h, c):
        inner = dot(kk_ref[h, c], rights[h, c])
        for r, cc, k in ((0, 0, 0), (0, 1, 2), (1, 1, 1)):
            tile = inner[r * HEAD : (r + 1) * HEAD, cc * HEAD : (cc + 1) * HEAD]
            high, low = split(tile * causal_ref[h, c, k])
            lanes = slice((r + cc) * HEAD, (r + cc + 1) * HEAD)
            inners[h, c, :HEAD, lanes] = high
            inners[h, c, HEAD:, lanes] = low

    def stage3(i, h, c):
        image = dot(state[h, c], rights[h, c])
        image = image[:HEAD] + image[HEAD:] + dot(kt_ref[h, c, :, :CHUNK], inners[h, c, :, :CHUNK])
        late = dot(kt_ref[h, c, :, CHUNK:], inners[h, c, :, CHUNK:])
        step = coef_ref[h, pl.ds(i, 1), span_of(c)]
        for k in range(CHUNK // HEAD):
            lanes = slice(k * HEAD, (k + 1) * HEAD)
            span = slice(c * CHUNK + k * HEAD, c * CHUNK + (k + 1) * HEAD)
            part = image[:, lanes] + late if k else image[:, lanes]
            res[h, :, span] = res[h, :, span] - step[:, lanes] * (part + ridge_ref[first + h] * direction[h, :, span])

    def body(i, carry):
        for ch in chains:
            stage1(i, *ch)
        for ch in chains:
            stage2(i, *ch)
        for ch in chains:
            stage3(i, *ch)
        return carry

    lax.fori_loop(0, ITERS - 1, body, 0)
    for h, c in chains:
        advance(ITERS - 1, h, c)


def mix(heads, digit_ref, part_refs, solved_ref, kk_ref, rate_ref, vt_ref, vst_ref, gain_ref, outs):
    chunks = kk_ref.shape[1]
    per = outs[0].shape[0]
    keep = iota((CHUNK, CHUNK), 0) <= iota((CHUNK, CHUNK), 1)
    for h in range(heads):
        prior = gathered(digit_ref, part_refs, h, slice(PACKED, BOTH))
        gain = jnp.broadcast_to(gain_ref[:, head_cols(h)], (HEAD, HEAD)).T
        for c in range(chunks):
            span = slice(c * CHUNK, (c + 1) * CHUNK)
            right = jnp.concatenate(split(solved_ref[h, :, span]), 0)
            inner = dot(kk_ref[h, c], right)
            by = rate_ref[h, span]
            high, low = split(jnp.where(keep, inner * jnp.concatenate([by, by], 1), 0.0))
            mixed = dot(stack_state(prior if c == 0 else prior + vst_ref[h, c - 1]), right)
            vals = vt_ref[h, :, span]
            mixed = mixed[:HEAD] + mixed[HEAD:] + dot(vals, high) + dot(vals, low)
            normed = mixed * lax.rsqrt(jnp.mean(mixed * mixed, axis=0, keepdims=True) + EPS)
            normed = normed * jnp.concatenate([gain] * (CHUNK // HEAD), 1)
            outs[h // per][h % per, :, span] = normed.astype(BF16)


def attend_kernel(base_ref, query_ref, rim_ref, ko_ref, vo_ref, after_ref, out_ref, kk, vv):
    rows, width = ko_ref.shape
    kk[:WINDOW] = rim_ref[:, :width]
    kk[WINDOW:] = ko_ref[...]
    vv[:, :WINDOW] = rim_ref[:, width:].astype(F32).T.astype(BF16)
    vv[:, WINDOW:] = vo_ref[...].astype(F32).T.astype(BF16)
    bias = jnp.where(base_ref[0] > 0, 0.0, FAR).astype(F32)
    key_at, query_at = iota((HEAD, HEAD), 0), iota((HEAD, HEAD), 1)
    tiles = WINDOW // HEAD
    scale = 1.0 / math.sqrt(HEAD)
    for h in range(query_ref.shape[0]):
        for j in range(rows // HEAD):
            near = slice(j * HEAD, (j + tiles + 1) * HEAD)
            scores = dot(kk[near], query_ref[h, :, j * HEAD : (j + 1) * HEAD])
            pieces = []
            for t in range(tiles + 1):
                piece = scores[t * HEAD : (t + 1) * HEAD]
                if t == 0:
                    piece = jnp.where(key_at > query_at, piece, FAR)
                if t == tiles:
                    piece = jnp.where(key_at <= query_at, piece, FAR)
                if j + t < tiles:
                    piece = piece + bias
                pieces.append(piece)
            scores = jnp.concatenate(pieces, 0)
            peak = jnp.max(scores, axis=0, keepdims=True)
            grown = jnp.exp((scores - peak) * scale)
            share = 1.0 / jnp.sum(grown, axis=0, keepdims=True)
            mixed_vals = dot(vv[:, near], (grown * share).astype(BF16))
            out_ref[j * HEAD : (j + 1) * HEAD, head_cols(h)] = mixed_vals.T.astype(BF16)


def solve_kernel(heads, parts, groups, digit_ref, base_ref, ridge_ref, *refs):
    part_refs, refs = refs[:parts], refs[parts:]
    q_ref, k_ref, v_ref, gain_ref = refs[:4]
    outs, refs = refs[4 : 4 + groups], refs[4 + groups :]
    kk, kt, vt, kst, vst, coef, rates, causal, solved, state, res, way, rights, inners = refs
    prepare(heads, 0, base_ref, ridge_ref, q_ref, k_ref, v_ref, kk, kt, res, vt, kst, vst, coef, rates, causal)
    chebyshev(
        heads, 0, digit_ref, ridge_ref, part_refs,
        kk, kt, kst, coef, causal, solved, state, res, way, rights, inners,
    )
    mix(heads, digit_ref, part_refs, solved, kk, rates, vt, vst, gain_ref, outs)


def project_kernel(groups, count, *refs):
    out_ref = refs[-1]
    total = None
    for g in range(groups):
        for i in range(count):
            left = refs[g * count + i]
            width = left.shape[1]
            part = dot(left[...], refs[groups * count + i][g * width : (g + 1) * width])
            total = part if total is None else total + part
    out_ref[...] = total.astype(BF16)


SMEM = pl.BlockSpec(memory_space=pltpu.SMEM)
VMEM = pl.BlockSpec(memory_space=pltpu.VMEM)


def call(kernel, outs, args, scalars=0, scratch=(), flops=0, nbytes=0):
    return pl.pallas_call(
        kernel,
        out_shape=outs,
        in_specs=[SMEM] * scalars + [VMEM] * (len(args) - scalars),
        out_specs=jax.tree.map(lambda _: VMEM, outs),
        scratch_shapes=list(scratch),
        compiler_params=pltpu.CompilerParams(vmem_limit_bytes=28 * 1024 * 1024),
        cost_estimate=pl.CostEstimate(flops=flops, bytes_accessed=nbytes, transcendentals=0),
    )(*args)


def rounds_of(count, stride):
    rounds = []
    while stride < count:
        left = count // stride
        radix = 4 if left % 4 == 0 else 2 if left % 2 == 0 else left
        rounds.append((stride, radix))
        stride *= radix
    return rounds


def partner(i, stride, radix, k):
    digit = (i // stride) % radix
    other = digit ^ k if radix in (2, 4) else (digit + k) % radix
    return i + (other - digit) * stride


def swap(x, axis, stride, radix, k):
    n = lax.axis_size(axis)
    return lax.ppermute(x, axis, [(i, partner(i, stride, radix, k)) for i in range(n)])


def source_digit(mine, stride, radix, k):
    digit = (mine // stride) % radix
    return digit ^ k if radix in (2, 4) else (digit - k) % radix


def before_flags(axis, first):
    mine = lax.axis_index(axis)
    flags = [mine < 0]
    for stride, radix in rounds_of(lax.axis_size(axis), first):
        digit = (mine // stride) % radix
        flags += [source_digit(mine, stride, radix, k) < digit for k in range(1, radix)]
    return jnp.stack(flags[1:] or flags).astype(jnp.int32)


def shards(
    mixer_queries, mixer_keys, mixer_values, window_keys, window_values, out_gain, ridge, out_weight
):
    rows = mixer_queries.shape[0]
    heads = ridge.shape[0]
    chunks = rows // CHUNK
    seq, head = lax.axis_size("seq"), lax.axis_size("head")
    base = (lax.axis_index("seq") * rows).astype(jnp.int32).reshape(1)
    shares = next(n for n in (4, 2, 1) if heads % n == 0 and seq % n == 0)
    own = heads // shares
    digit = (lax.axis_index("seq") % shares).astype(jnp.int32).reshape(1)
    flags = before_flags("seq", shares)
    per = heads // GROUPS
    shape = jax.ShapeDtypeStruct
    width = window_keys.shape[1]
    block = shape((own, BOTH, HEAD), F32)

    def traded(parts):
        return [parts[0]] + [swap(parts[k], "seq", 1, shares, k) for k in range(1, shares)]

    rim = jnp.concatenate([window_keys, window_values], 1)[rows - WINDOW :]
    moments = call(
        functools.partial(moments_kernel, shares),
        (block,) * shares,
        (digit, mixer_keys, mixer_values),
        scalars=1,
    )
    moments = traded(moments)
    total = functools.reduce(jnp.add, moments)
    total, rim, out_weight = lax.optimization_barrier((total, rim, out_weight))
    mine = lax.axis_index("head")
    cols = out_weight.shape[1] // head
    rights = []
    for k in range(head):
        piece = lax.dynamic_slice_in_dim(out_weight, partner(mine, 1, head, k) * cols, cols, 1)
        rights.append(piece if k == 0 else swap(piece, "head", 1, head, k))
    common = jnp.zeros_like(total)
    rounds = rounds_of(seq, shares)
    i = 0
    for at, (stride, radix) in enumerate(rounds):
        got = [swap(total, "seq", stride, radix, k) for k in range(1, radix)]
        for part in got:
            common = common + jnp.where(flags[i] > 0, part, 0.0)
            i += 1
        if at + 1 < len(rounds):
            total = functools.reduce(jnp.add, got, total)
    priors = []
    for k in range(shares):
        prior = common
        for j in range(shares):
            if j != k:
                prior = prior + jnp.where((digit[0] ^ j) < (digit[0] ^ k), moments[j], 0.0)
        priors.append(prior)
    priors = traded(priors)
    priors, rim = lax.optimization_barrier((priors, rim))
    rim = lax.ppermute(rim, "seq", [(i, (i + 1) % seq) for i in range(seq)])

    queries = call(
        functools.partial(solve_kernel, heads, shares, GROUPS),
        (shape((per, HEAD, rows), BF16),) * GROUPS,
        (
            digit, base, ridge, *priors, mixer_queries, mixer_keys, mixer_values,
            out_gain.reshape(1, -1),
        ),
        scalars=3,
        scratch=(
            pltpu.VMEM((heads, chunks, CHUNK, 2 * HEAD), BF16),
            pltpu.VMEM((heads, chunks, HEAD, 2 * CHUNK), BF16),
            pltpu.VMEM((heads, HEAD, rows), BF16),
            pltpu.VMEM((heads, chunks - 1, HEAD, HEAD), F32),
            pltpu.VMEM((heads, chunks - 1, HEAD, HEAD), F32),
            pltpu.VMEM((heads, 2 * ITERS, rows), F32),
            pltpu.VMEM((heads, rows, HEAD), F32),
            pltpu.VMEM((heads, chunks, 3, HEAD, HEAD), F32),
            pltpu.VMEM((heads, HEAD, rows), F32),
            *cheb_scratch(heads, chunks),
        ),
        flops=10**10,
        nbytes=3 * 10**7,
    )
    lefts = []
    after = rim
    for g in range(GROUPS):
        (attended,) = call(
            attend_kernel,
            (shape((rows, per * HEAD), BF16),),
            (base, queries[g], rim, window_keys, window_values, after),
            scalars=1,
            scratch=(pltpu.VMEM((WINDOW + rows, width), BF16), pltpu.VMEM((width, WINDOW + rows), BF16)),
            flops=4 * 10**9,
            nbytes=15 * 10**6,
        )
        after = attended
        if head == 4:
            far = swap(attended, "head", 1, 4, 2)
            lefts += [attended, swap(attended, "head", 1, 4, 1), far, swap(far, "head", 1, 4, 1)]
        else:
            lefts += [attended] + [swap(attended, "head", 1, head, k) for k in range(1, head)]
    return call(
        functools.partial(project_kernel, GROUPS, head),
        shape((rows, cols), BF16),
        (*lefts, *rights),
    )


def solution(mesh):
    return jax.shard_map(
        shards,
        mesh=mesh,
        in_specs=(
            P("seq", "head"),
            P("seq", "head"),
            P("seq", "head"),
            P("seq", "head"),
            P("seq", "head"),
            P("head"),
            P("head"),
            P("head", None),
        ),
        out_specs=P("seq", "head"),
        check_vma=False,
    )
```

```python
import functools
import math

import jax
import jax.numpy as jnp
from jax import lax
from jax.experimental import pallas as pl
from jax.experimental.pallas import tpu as pltpu
from jax.sharding import PartitionSpec as P

ITERS = 8
WINDOW = 512
EPS = 1e-06
HEAD = 128
HALF = HEAD // 2
CHUNK = 256
PACKED = HALF + 8
BOTH = PACKED + HEAD
FAR = -1e30
F32 = jnp.float32
BF16 = jnp.bfloat16


def dot(a, b):
    return jnp.dot(a, b, preferred_element_type=F32)


def split(x):
    high = x.astype(BF16)
    return high, (x - high.astype(F32)).astype(BF16)


def rate(x):
    return lax.rsqrt(jnp.mean(x * x, axis=-1, keepdims=True) + EPS) * (1.0 / math.sqrt(HEAD))


def unit(x):
    x = x.astype(F32)
    return x * rate(x)


def iota(shape, dim):
    return lax.broadcasted_iota(jnp.int32, shape, dim)


def head_cols(h):
    return slice(h * HEAD, (h + 1) * HEAD)


def pack(m):
    top, low = m[:HALF], pltpu.roll(m[HALF:], HALF, 1)
    row, col = iota((HALF, HEAD), 0), iota((HALF, HEAD), 1)
    body = jnp.where((col >= HALF) | (row > col), top, low)
    diag = jnp.sum(jnp.where(row == col, top, 0.0), axis=0, keepdims=True)
    return body, jnp.broadcast_to(diag, (8, HEAD))


def unpack(p):
    body, diag = p[:HALF], p[HALF : HALF + 1]
    row, col = iota((HALF, HEAD), 0), iota((HALF, HEAD), 1)
    top = jnp.where((col >= HALF) | (row > col), body, 0.0) + jnp.where(row == col, 0.5 * diag, 0.0)
    low = jnp.where((col < HALF) & (row <= col), body, 0.0) * jnp.where(row == col, 0.5, 1.0)
    half = jnp.concatenate([top, pltpu.roll(low, HALF, 1)], 0)
    return half + half.T


def group_sizes(heads):
    return [heads - heads // 2, heads // 2] if heads > 1 else [1]


def moments_kernel(shares, digit_ref, keys_ref, vals_ref, *outs):
    own = outs[0].shape[0]
    for k in range(shares):
        for j in range(own):
            cols = pl.ds(pl.multiple_of(((digit_ref[0] ^ k) * own + j) * HEAD, HEAD), HEAD)
            keys = keys_ref[:, cols].astype(F32)
            scale = rate(keys)
            once = keys * scale
            pair = dot(keys.T.astype(BF16), jnp.concatenate(split(once * scale), 1))
            body, diag = pack(pair[:, :HEAD] + pair[:, HEAD:])
            outs[k][j, :HALF] = body
            outs[k][j, HALF:PACKED] = diag
            vals_t = vals_ref[:, cols].astype(F32).T.astype(BF16)
            pair = dot(vals_t, jnp.concatenate(split(once), 1))
            outs[k][j, PACKED:] = pair[:, :HEAD] + pair[:, HEAD:]


def prepare(heads, first, base_ref, ridge_ref, q_ref, k_ref, v_ref, *outs):
    rows = q_ref.shape[0]
    chunks = rows // CHUNK
    kk_ref, kt_ref, qt_ref, vt_ref, kst_ref, vst_ref, coef_ref, rate_ref, causal_ref = outs
    keep = iota((HEAD, HEAD), 0) <= iota((HEAD, HEAD), 1)
    for h in range(heads):
        cols = head_cols(first + h)
        raw = k_ref[:, cols]
        keys = raw.astype(F32)
        scale = rate(keys)
        square = jnp.broadcast_to(scale * scale, keys.shape)
        rate_ref[h] = jnp.broadcast_to(scale, keys.shape)
        keys_t = keys.T.astype(BF16)
        once = jnp.concatenate(split(keys * scale), 1)
        twice = jnp.concatenate(split(keys * square), 1)
        vals_t = v_ref[:, cols].astype(F32).T.astype(BF16)
        vt_ref[h] = vals_t
        qt_ref[h] = unit(q_ref[:, cols]).T
        key_sum = val_sum = None
        for c in range(chunks):
            span = slice(c * CHUNK, (c + 1) * CHUNK)
            if c:
                kst_ref[h, c - 1] = key_sum
                vst_ref[h, c - 1] = val_sum
            kk_ref[h, c] = jnp.concatenate([raw[span], raw[span]], 1)
            for r in range(CHUNK // HEAD):
                at = slice(c * CHUNK + r * HEAD, c * CHUNK + (r + 1) * HEAD)
                kt_ref[h, c, :, 2 * r * HEAD : (2 * r + 2) * HEAD] = jnp.concatenate([keys_t[:, at]] * 2, 1)
                across = jnp.where(keep, square[at], 0.0)
                causal_ref[h, c, r] = across
                if r == 0:
                    causal_ref[h, c, 2] = square[at]
            if c + 1 < chunks:
                mv = dot(vals_t[:, span], once[span])
                mv = mv[:, :HEAD] + mv[:, HEAD:]
                val_sum = mv if c == 0 else val_sum + mv
                mk = dot(keys_t[:, span], twice[span])
                mk = mk[:, :HEAD] + mk[:, HEAD:]
                key_sum = mk if c == 0 else key_sum + mk
        ridge = ridge_ref[first + h]
        places = (iota((1, rows), 1) + (base_ref[0] + 1)).astype(F32)
        upper = ridge + places
        centre = (upper + ridge) * 0.5
        radius = (upper - ridge) * 0.5
        step = 1.0 / centre
        weight = jnp.zeros_like(step)
        for i in range(ITERS):
            if i:
                scaled = radius * step
                weight = scaled * scaled * (0.5 if i == 1 else 0.25)
                step = 1.0 / (centre - weight / step)
            coef_ref[h, i : i + 1] = step
            coef_ref[h, ITERS + i : ITERS + i + 1] = weight


def gathered(digit_ref, part_refs, h, rows):
    own = part_refs[0].shape[0]
    total = None
    for k, ref in enumerate(part_refs):
        part = jnp.where((digit_ref[0] ^ k) == h // own, ref[h % own, rows], 0.0)
        total = part if total is None else total + part
    return total


def stack_state(state):
    high, low = split(state)
    return jnp.concatenate(
        [jnp.concatenate([high, high], 1), jnp.concatenate([low, low], 1)], 0
    )


def cheb_scratch(per, chunks):
    return (
        pltpu.VMEM((per, chunks, 2 * HEAD, 2 * HEAD), BF16),
        pltpu.VMEM((per, HEAD, chunks * CHUNK), F32),
        pltpu.VMEM((per, HEAD, chunks * CHUNK), F32),
        pltpu.VMEM((per, chunks, 2 * HEAD, CHUNK), BF16),
        pltpu.VMEM((per, chunks, CHUNK, CHUNK + HEAD), BF16),
    )


def chebyshev(heads, first, digit_ref, ridge_ref, part_refs, *refs):
    kk_ref, kt_ref, kst_ref, coef_ref, causal_ref, solved_ref, state, res, direction, rights, inners = refs
    chunks = kk_ref.shape[1]
    for h in range(heads):
        prior = unpack(gathered(digit_ref, part_refs, first + h, slice(0, PACKED)))
        for c in range(chunks):
            state[h, c] = stack_state(prior if c == 0 else prior + kst_ref[h, c - 1])
        direction[h] = jnp.zeros_like(direction[h])
        solved_ref[h] = jnp.zeros_like(solved_ref[h])
    chains = [(h, c) for h in range(heads) for c in range(chunks)]

    def span_of(c):
        return slice(c * CHUNK, (c + 1) * CHUNK)

    def advance(i, h, c):
        span = span_of(c)
        step = coef_ref[h, pl.ds(i, 1), span]
        weight = coef_ref[h, pl.ds(ITERS + i, 1), span]
        way = res[h, :, span] + weight * direction[h, :, span]
        solved_ref[h, :, span] = solved_ref[h, :, span] + step * way
        return way

    def stage1(i, h, c):
        way = advance(i, h, c)
        direction[h, :, span_of(c)] = way
        high, low = split(way)
        rights[h, c, :HEAD] = high
        rights[h, c, HEAD:] = low

    def stage2(i, h, c):
        inner = dot(kk_ref[h, c], rights[h, c])
        for r, cc, k in ((0, 0, 0), (0, 1, 2), (1, 1, 1)):
            tile = inner[r * HEAD : (r + 1) * HEAD, cc * HEAD : (cc + 1) * HEAD]
            high, low = split(tile * causal_ref[h, c, k])
            lanes = slice((r + cc) * HEAD, (r + cc + 1) * HEAD)
            inners[h, c, :HEAD, lanes] = high
            inners[h, c, HEAD:, lanes] = low

    def stage3(i, h, c):
        image = dot(state[h, c], rights[h, c])
        image = image[:HEAD] + image[HEAD:] + dot(kt_ref[h, c, :, :CHUNK], inners[h, c, :, :CHUNK])
        late = dot(kt_ref[h, c, :, CHUNK:], inners[h, c, :, CHUNK:])
        step = coef_ref[h, pl.ds(i, 1), span_of(c)]
        for k in range(CHUNK // HEAD):
            lanes = slice(k * HEAD, (k + 1) * HEAD)
            span = slice(c * CHUNK + k * HEAD, c * CHUNK + (k + 1) * HEAD)
            part = image[:, lanes] + late if k else image[:, lanes]
            res[h, :, span] = res[h, :, span] - step[:, lanes] * (part + ridge_ref[first + h] * direction[h, :, span])

    def body(i, carry):
        for ch in chains:
            stage1(i, *ch)
        for ch in chains:
            stage2(i, *ch)
        for ch in chains:
            stage3(i, *ch)
        return carry

    lax.fori_loop(0, ITERS - 1, body, 0)
    for h, c in chains:
        advance(ITERS - 1, h, c)


def mix(heads, first, digit_ref, part_refs, solved_ref, kk_ref, rate_ref, vt_ref, vst_ref, gain_ref, out_ref):
    chunks = kk_ref.shape[1]
    keep = iota((CHUNK, CHUNK), 0) <= iota((CHUNK, CHUNK), 1)
    for h in range(heads):
        prior = gathered(digit_ref, part_refs, first + h, slice(PACKED, BOTH))
        gain = jnp.broadcast_to(gain_ref[:, head_cols(first + h)], (HEAD, HEAD)).T
        for c in range(chunks):
            span = slice(c * CHUNK, (c + 1) * CHUNK)
            right = jnp.concatenate(split(solved_ref[h, :, span]), 0)
            inner = dot(kk_ref[h, c], right)
            by = rate_ref[h, span]
            high, low = split(jnp.where(keep, inner * jnp.concatenate([by, by], 1), 0.0))
            mixed = dot(stack_state(prior if c == 0 else prior + vst_ref[h, c - 1]), right)
            vals = vt_ref[h, :, span]
            mixed = mixed[:HEAD] + mixed[HEAD:] + dot(vals, high) + dot(vals, low)
            normed = mixed * lax.rsqrt(jnp.mean(mixed * mixed, axis=0, keepdims=True) + EPS)
            normed = normed * jnp.concatenate([gain] * (CHUNK // HEAD), 1)
            out_ref[h, :, span] = normed.astype(BF16)


def attend_kernel(base_ref, query_ref, rim_ref, ko_ref, vo_ref, after_ref, out_ref, kk, vv):
    rows, width = ko_ref.shape
    kk[:WINDOW] = rim_ref[:, :width]
    kk[WINDOW:] = ko_ref[...]
    vv[:, :WINDOW] = rim_ref[:, width:].astype(F32).T.astype(BF16)
    vv[:, WINDOW:] = vo_ref[...].astype(F32).T.astype(BF16)
    bias = jnp.where(base_ref[0] > 0, 0.0, FAR).astype(F32)
    key_at, query_at = iota((HEAD, HEAD), 0), iota((HEAD, HEAD), 1)
    tiles = WINDOW // HEAD
    scale = 1.0 / math.sqrt(HEAD)
    for h in range(query_ref.shape[0]):
        for j in range(rows // HEAD):
            near = slice(j * HEAD, (j + tiles + 1) * HEAD)
            scores = dot(kk[near], query_ref[h, :, j * HEAD : (j + 1) * HEAD])
            pieces = []
            for t in range(tiles + 1):
                piece = scores[t * HEAD : (t + 1) * HEAD]
                if t == 0:
                    piece = jnp.where(key_at > query_at, piece, FAR)
                if t == tiles:
                    piece = jnp.where(key_at <= query_at, piece, FAR)
                if j + t < tiles:
                    piece = piece + bias
                pieces.append(piece)
            scores = jnp.concatenate(pieces, 0)
            peak = jnp.max(scores, axis=0, keepdims=True)
            grown = jnp.exp((scores - peak) * scale)
            share = 1.0 / jnp.sum(grown, axis=0, keepdims=True)
            mixed_vals = dot(vv[:, near], (grown * share).astype(BF16))
            out_ref[j * HEAD : (j + 1) * HEAD, head_cols(h)] = mixed_vals.T.astype(BF16)


def solve_kernel(heads, parts, first, digit_ref, base_ref, ridge_ref, *refs):
    part_refs, refs = refs[:parts], refs[parts:]
    q_ref, k_ref, v_ref, gain_ref, after_ref, out_ref, *refs = refs
    kk, kt, vt, kst, vst, coef, rates, causal, solved, state, res, way, rights, inners = refs
    prepare(heads, first, base_ref, ridge_ref, q_ref, k_ref, v_ref, kk, kt, res, vt, kst, vst, coef, rates, causal)
    chebyshev(
        heads, first, digit_ref, ridge_ref, part_refs,
        kk, kt, kst, coef, causal, solved, state, res, way, rights, inners,
    )
    mix(heads, first, digit_ref, part_refs, solved, kk, rates, vt, vst, gain_ref, out_ref)


def project_kernel(pairs, count, *refs):
    out_ref, last = refs[-1], refs[-2][...] if len(refs) > count + 1 else None
    for left, right, row in pairs:
        part = dot(refs[left][...], refs[right][row : row + refs[left].shape[1]])
        last = part if last is None else last + part
    out_ref[...] = last.astype(out_ref.dtype)


SMEM = pl.BlockSpec(memory_space=pltpu.SMEM)
VMEM = pl.BlockSpec(memory_space=pltpu.VMEM)


def call(kernel, outs, args, scalars=0, scratch=(), flops=0, nbytes=0):
    return pl.pallas_call(
        kernel,
        out_shape=outs,
        in_specs=[SMEM] * scalars + [VMEM] * (len(args) - scalars),
        out_specs=jax.tree.map(lambda _: VMEM, outs),
        scratch_shapes=list(scratch),
        compiler_params=pltpu.CompilerParams(vmem_limit_bytes=28 * 1024 * 1024),
        cost_estimate=pl.CostEstimate(flops=flops, bytes_accessed=nbytes, transcendentals=0),
    )(*args)


def rounds_of(count, stride):
    rounds = []
    while stride < count:
        left = count // stride
        radix = 4 if left % 4 == 0 else 2 if left % 2 == 0 else left
        rounds.append((stride, radix))
        stride *= radix
    return rounds


def partner(i, stride, radix, k):
    digit = (i // stride) % radix
    other = digit ^ k if radix in (2, 4) else (digit + k) % radix
    return i + (other - digit) * stride


def swap(x, axis, stride, radix, k):
    n = lax.axis_size(axis)
    return lax.ppermute(x, axis, [(i, partner(i, stride, radix, k)) for i in range(n)])


def source_digit(mine, stride, radix, k):
    digit = (mine // stride) % radix
    return digit ^ k if radix in (2, 4) else (digit - k) % radix


def before_flags(axis, first):
    mine = lax.axis_index(axis)
    flags = [mine < 0]
    for stride, radix in rounds_of(lax.axis_size(axis), first):
        digit = (mine // stride) % radix
        flags += [source_digit(mine, stride, radix, k) < digit for k in range(1, radix)]
    return jnp.stack(flags[1:] or flags).astype(jnp.int32)


def shards(
    mixer_queries, mixer_keys, mixer_values, window_keys, window_values, out_gain, ridge, out_weight
):
    rows = mixer_queries.shape[0]
    heads = ridge.shape[0]
    chunks = rows // CHUNK
    seq, head = lax.axis_size("seq"), lax.axis_size("head")
    base = (lax.axis_index("seq") * rows).astype(jnp.int32).reshape(1)
    shares = next(n for n in (4, 2, 1) if heads % n == 0 and seq % n == 0)
    own = heads // shares
    digit = (lax.axis_index("seq") % shares).astype(jnp.int32).reshape(1)
    flags = before_flags("seq", shares)
    sizes = group_sizes(heads)
    shape = jax.ShapeDtypeStruct
    width = window_keys.shape[1]
    block = shape((own, BOTH, HEAD), F32)

    def traded(parts):
        return [parts[0]] + [swap(parts[k], "seq", 1, shares, k) for k in range(1, shares)]

    rim = jnp.concatenate([window_keys, window_values], 1)[rows - WINDOW :]
    moments = call(
        functools.partial(moments_kernel, shares),
        (block,) * shares,
        (digit, mixer_keys, mixer_values),
        scalars=1,
    )
    moments = traded(moments)
    total = functools.reduce(jnp.add, moments)
    mine = lax.axis_index("head")
    cols = out_weight.shape[1] // head
    def columns(x, block, count=1):
        return lax.dynamic_slice_in_dim(x, block * cols, count * cols, 1)

    w_far = rim
    if head == 4:
        core = mine % 2
        near = swap(columns(out_weight, mine ^ 1), "head", 1, 4, 1)
        w_far = swap(columns(out_weight, (mine // 2 ^ 1) * 2, 2), "head", 1, 4, 2)
        relayed = swap(columns(w_far, core ^ 1), "head", 1, 4, 1)
        rights = [columns(out_weight, mine), near, columns(w_far, core), relayed]
    else:
        rights = [columns(out_weight, mine)]
        rights += [swap(columns(out_weight, partner(mine, 1, head, k)), "head", 1, head, k) for k in range(1, head)]
    common = jnp.zeros_like(total)
    rounds = rounds_of(seq, shares)
    i = 0
    for at, (stride, radix) in enumerate(rounds):
        got = [swap(total, "seq", stride, radix, k) for k in range(1, radix)]
        for part in got:
            common = common + jnp.where(flags[i] > 0, part, 0.0)
            i += 1
        if at + 1 < len(rounds):
            total = functools.reduce(jnp.add, got, total)
    priors = []
    for k in range(shares):
        prior = common
        for j in range(shares):
            if j != k:
                prior = prior + jnp.where((digit[0] ^ j) < (digit[0] ^ k), moments[j], 0.0)
        priors.append(prior)
    priors = traded(priors)
    rim = lax.ppermute(rim, "seq", [(i, (i + 1) % seq) for i in range(seq)])

    lefts = []
    attended, far = rim, w_far
    first = 0
    for per in sizes:
        (queries,) = call(
            functools.partial(solve_kernel, per, shares, first),
            (shape((per, HEAD, rows), BF16),),
            (
                digit, base, ridge, *priors, mixer_queries, mixer_keys, mixer_values,
                out_gain.reshape(1, -1), attended if first else out_gain.reshape(1, -1),
            ),
            scalars=3,
            scratch=(
                pltpu.VMEM((per, chunks, CHUNK, 2 * HEAD), BF16),
                pltpu.VMEM((per, chunks, HEAD, 2 * CHUNK), BF16),
                pltpu.VMEM((per, HEAD, rows), BF16),
                pltpu.VMEM((per, chunks - 1, HEAD, HEAD), F32),
                pltpu.VMEM((per, chunks - 1, HEAD, HEAD), F32),
                pltpu.VMEM((per, 2 * ITERS, rows), F32),
                pltpu.VMEM((per, rows, HEAD), F32),
                pltpu.VMEM((per, chunks, 3, HEAD, HEAD), F32),
                pltpu.VMEM((per, HEAD, rows), F32),
                *cheb_scratch(per, chunks),
            ),
            flops=10**10,
            nbytes=3 * 10**7,
        )
        (attended,) = call(
            attend_kernel,
            (shape((rows, per * HEAD), BF16),),
            (base, queries, rim, window_keys, window_values, far),
            scalars=1,
            scratch=(pltpu.VMEM((WINDOW + rows, width), BF16), pltpu.VMEM((width, WINDOW + rows), BF16)),
            flops=4 * 10**9,
            nbytes=15 * 10**6,
        )
        first += per
        if head == 4:
            far = swap(attended, "head", 1, 4, 2)
            lefts += [attended, swap(attended, "head", 1, 4, 1), far, swap(far, "head", 1, 4, 1)]
        else:
            lefts += [attended] + [swap(attended, "head", 1, head, k) for k in range(1, head)]
    def project(chosen, kind, *more):
        left = [lefts[g * head + k] for g, k in chosen]
        rows_of = [sum(sizes[:g]) * HEAD for g, _ in chosen]
        right = [rights[k] for _, k in chosen]
        count = 2 * len(chosen)
        pairs = [(i, len(chosen) + i, row) for i, row in enumerate(rows_of)]
        return call(
            functools.partial(project_kernel, pairs, count),
            (shape((rows, cols), kind),),
            (*left, *right, *more),
        )[0]

    last = len(sizes) - 1
    early = [(g, k) for g in range(len(sizes)) for k in range(head) if g < last or k < 2]
    late = [(last, k) for k in range(2, head)]
    if not late:
        return project(early, BF16)
    return project(late, BF16, project(early, F32))


def solution(mesh):
    return jax.shard_map(
        shards,
        mesh=mesh,
        in_specs=(
            P("seq", "head"),
            P("seq", "head"),
            P("seq", "head"),
            P("seq", "head"),
            P("seq", "head"),
            P("head"),
            P("head"),
            P("head", None),
        ),
        out_specs=P("seq", "head"),
        check_vma=False,
    )
```

```python
import functools
import math

import jax
import jax.numpy as jnp
from jax import lax
from jax.experimental import pallas as pl
from jax.experimental.pallas import tpu as pltpu
from jax.sharding import PartitionSpec as P

ITERS = 8
WINDOW = 512
EPS = 1e-06
HEAD = 128
HALF = HEAD // 2
CHUNK = 256
PACKED = HALF + 8
BOTH = PACKED + HEAD
FAR = -1e30
F32 = jnp.float32
BF16 = jnp.bfloat16


def dot(a, b):
    return jnp.dot(a, b, preferred_element_type=F32)


def split(x):
    high = x.astype(BF16)
    return high, (x - high.astype(F32)).astype(BF16)


def rate(x):
    return lax.rsqrt(jnp.mean(x * x, axis=-1, keepdims=True) + EPS) * (1.0 / math.sqrt(HEAD))


def unit(x):
    x = x.astype(F32)
    return x * rate(x)


def iota(shape, dim):
    return lax.broadcasted_iota(jnp.int32, shape, dim)


def head_cols(h):
    return slice(h * HEAD, (h + 1) * HEAD)


def pack(m):
    top, low = m[:HALF], pltpu.roll(m[HALF:], HALF, 1)
    row, col = iota((HALF, HEAD), 0), iota((HALF, HEAD), 1)
    body = jnp.where((col >= HALF) | (row > col), top, low)
    diag = jnp.sum(jnp.where(row == col, top, 0.0), axis=0, keepdims=True)
    return body, jnp.broadcast_to(diag, (8, HEAD))


def unpack(p):
    body, diag = p[:HALF], p[HALF : HALF + 1]
    row, col = iota((HALF, HEAD), 0), iota((HALF, HEAD), 1)
    top = jnp.where((col >= HALF) | (row > col), body, 0.0) + jnp.where(row == col, 0.5 * diag, 0.0)
    low = jnp.where((col < HALF) & (row <= col), body, 0.0) * jnp.where(row == col, 0.5, 1.0)
    half = jnp.concatenate([top, pltpu.roll(low, HALF, 1)], 0)
    return half + half.T


def group_sizes(heads):
    return [heads - heads // 2, heads // 2] if heads > 1 else [1]


def moments_kernel(shares, digit_ref, keys_ref, vals_ref, *outs):
    own = outs[0].shape[0]
    for k in range(shares):
        for j in range(own):
            cols = pl.ds(pl.multiple_of(((digit_ref[0] ^ k) * own + j) * HEAD, HEAD), HEAD)
            keys = keys_ref[:, cols].astype(F32)
            scale = rate(keys)
            once = keys * scale
            pair = dot(keys.T.astype(BF16), jnp.concatenate(split(once * scale), 1))
            body, diag = pack(pair[:, :HEAD] + pair[:, HEAD:])
            outs[k][j, :HALF] = body
            outs[k][j, HALF:PACKED] = diag
            vals_t = vals_ref[:, cols].astype(F32).T.astype(BF16)
            pair = dot(vals_t, jnp.concatenate(split(once), 1))
            outs[k][j, PACKED:] = pair[:, :HEAD] + pair[:, HEAD:]


def prepare(heads, first, base_ref, ridge_ref, q_ref, k_ref, v_ref, *outs):
    rows = q_ref.shape[0]
    chunks = rows // CHUNK
    kk_ref, kt_ref, qt_ref, vt_ref, kst_ref, vst_ref, coef_ref, rate_ref, causal_ref = outs
    keep = iota((HEAD, HEAD), 0) <= iota((HEAD, HEAD), 1)
    for h in range(heads):
        cols = head_cols(first + h)
        raw = k_ref[:, cols]
        keys = raw.astype(F32)
        scale = rate(keys)
        square = jnp.broadcast_to(scale * scale, keys.shape)
        rate_ref[h] = jnp.broadcast_to(scale, keys.shape)
        keys_t = keys.T.astype(BF16)
        once = jnp.concatenate(split(keys * scale), 1)
        twice = jnp.concatenate(split(keys * square), 1)
        vals_t = v_ref[:, cols].astype(F32).T.astype(BF16)
        vt_ref[h] = vals_t
        qt_ref[h] = unit(q_ref[:, cols]).T
        key_sum = val_sum = None
        for c in range(chunks):
            span = slice(c * CHUNK, (c + 1) * CHUNK)
            if c:
                kst_ref[h, c - 1] = key_sum
                vst_ref[h, c - 1] = val_sum
            kk_ref[h, c] = jnp.concatenate([raw[span], raw[span]], 1)
            for r in range(CHUNK // HEAD):
                at = slice(c * CHUNK + r * HEAD, c * CHUNK + (r + 1) * HEAD)
                kt_ref[h, c, :, 2 * r * HEAD : (2 * r + 2) * HEAD] = jnp.concatenate([keys_t[:, at]] * 2, 1)
                across = jnp.where(keep, square[at], 0.0)
                causal_ref[h, c, r] = across
                if r == 0:
                    causal_ref[h, c, 2] = square[at]
            if c + 1 < chunks:
                mv = dot(vals_t[:, span], once[span])
                mv = mv[:, :HEAD] + mv[:, HEAD:]
                val_sum = mv if c == 0 else val_sum + mv
                mk = dot(keys_t[:, span], twice[span])
                mk = mk[:, :HEAD] + mk[:, HEAD:]
                key_sum = mk if c == 0 else key_sum + mk
        ridge = ridge_ref[first + h]
        places = (iota((1, rows), 1) + (base_ref[0] + 1)).astype(F32)
        upper = ridge + places
        centre = (upper + ridge) * 0.5
        radius = (upper - ridge) * 0.5
        step = 1.0 / centre
        weight = jnp.zeros_like(step)
        for i in range(ITERS):
            if i:
                scaled = radius * step
                weight = scaled * scaled * (0.5 if i == 1 else 0.25)
                step = 1.0 / (centre - weight / step)
            coef_ref[h, i : i + 1] = step
            coef_ref[h, ITERS + i : ITERS + i + 1] = weight


def gathered(digit_ref, part_refs, h, rows):
    own = part_refs[0].shape[0]
    total = None
    for k, ref in enumerate(part_refs):
        part = jnp.where((digit_ref[0] ^ k) == h // own, ref[h % own, rows], 0.0)
        total = part if total is None else total + part
    return total


def stack_state(state):
    high, low = split(state)
    return jnp.concatenate(
        [jnp.concatenate([high, high], 1), jnp.concatenate([low, low], 1)], 0
    )


def cheb_scratch(per, chunks):
    return (
        pltpu.VMEM((per, chunks, 2 * HEAD, 2 * HEAD), BF16),
        pltpu.VMEM((per, HEAD, chunks * CHUNK), F32),
        pltpu.VMEM((per, HEAD, chunks * CHUNK), F32),
        pltpu.VMEM((per, chunks, 2 * HEAD, CHUNK), BF16),
        pltpu.VMEM((per, chunks, CHUNK, CHUNK + HEAD), BF16),
    )


def chebyshev(heads, first, digit_ref, ridge_ref, part_refs, *refs):
    kk_ref, kt_ref, kst_ref, coef_ref, causal_ref, solved_ref, state, res, direction, rights, inners = refs
    chunks = kk_ref.shape[1]
    for h in range(heads):
        prior = unpack(gathered(digit_ref, part_refs, first + h, slice(0, PACKED)))
        for c in range(chunks):
            state[h, c] = stack_state(prior if c == 0 else prior + kst_ref[h, c - 1])
        direction[h] = jnp.zeros_like(direction[h])
        solved_ref[h] = jnp.zeros_like(solved_ref[h])
    chains = [(h, c) for h in range(heads) for c in range(chunks)]

    def span_of(c):
        return slice(c * CHUNK, (c + 1) * CHUNK)

    def advance(i, h, c):
        span = span_of(c)
        step = coef_ref[h, pl.ds(i, 1), span]
        weight = coef_ref[h, pl.ds(ITERS + i, 1), span]
        way = res[h, :, span] + weight * direction[h, :, span]
        solved_ref[h, :, span] = solved_ref[h, :, span] + step * way
        return way

    def stage1(i, h, c):
        way = advance(i, h, c)
        direction[h, :, span_of(c)] = way
        high, low = split(way)
        rights[h, c, :HEAD] = high
        rights[h, c, HEAD:] = low

    def stage2(i, h, c):
        inner = dot(kk_ref[h, c], rights[h, c])
        for r, cc, k in ((0, 0, 0), (0, 1, 2), (1, 1, 1)):
            tile = inner[r * HEAD : (r + 1) * HEAD, cc * HEAD : (cc + 1) * HEAD]
            high, low = split(tile * causal_ref[h, c, k])
            lanes = slice((r + cc) * HEAD, (r + cc + 1) * HEAD)
            inners[h, c, :HEAD, lanes] = high
            inners[h, c, HEAD:, lanes] = low

    def stage3(i, h, c):
        image = dot(state[h, c], rights[h, c])
        image = image[:HEAD] + image[HEAD:] + dot(kt_ref[h, c, :, :CHUNK], inners[h, c, :, :CHUNK])
        late = dot(kt_ref[h, c, :, CHUNK:], inners[h, c, :, CHUNK:])
        step = coef_ref[h, pl.ds(i, 1), span_of(c)]
        for k in range(CHUNK // HEAD):
            lanes = slice(k * HEAD, (k + 1) * HEAD)
            span = slice(c * CHUNK + k * HEAD, c * CHUNK + (k + 1) * HEAD)
            part = image[:, lanes] + late if k else image[:, lanes]
            res[h, :, span] = res[h, :, span] - step[:, lanes] * (part + ridge_ref[first + h] * direction[h, :, span])

    def body(i, carry):
        for ch in chains:
            stage1(i, *ch)
        for ch in chains:
            stage2(i, *ch)
        for ch in chains:
            stage3(i, *ch)
        return carry

    for i in range(ITERS - 1):
        body(i, 0)
    for h, c in chains:
        advance(ITERS - 1, h, c)


def mix(heads, first, digit_ref, part_refs, solved_ref, kk_ref, rate_ref, vt_ref, vst_ref, gain_ref, out_ref):
    chunks = kk_ref.shape[1]
    keep = iota((CHUNK, CHUNK), 0) <= iota((CHUNK, CHUNK), 1)
    for h in range(heads):
        prior = gathered(digit_ref, part_refs, first + h, slice(PACKED, BOTH))
        gain = jnp.broadcast_to(gain_ref[:, head_cols(first + h)], (HEAD, HEAD)).T
        for c in range(chunks):
            span = slice(c * CHUNK, (c + 1) * CHUNK)
            right = jnp.concatenate(split(solved_ref[h, :, span]), 0)
            inner = dot(kk_ref[h, c], right)
            by = rate_ref[h, span]
            high, low = split(jnp.where(keep, inner * jnp.concatenate([by, by], 1), 0.0))
            mixed = dot(stack_state(prior if c == 0 else prior + vst_ref[h, c - 1]), right)
            vals = vt_ref[h, :, span]
            mixed = mixed[:HEAD] + mixed[HEAD:] + dot(vals, high) + dot(vals, low)
            normed = mixed * lax.rsqrt(jnp.mean(mixed * mixed, axis=0, keepdims=True) + EPS)
            normed = normed * jnp.concatenate([gain] * (CHUNK // HEAD), 1)
            out_ref[h, :, span] = normed.astype(BF16)


def attend_kernel(base_ref, query_ref, rim_ref, ko_ref, vo_ref, after_ref, out_ref, kk, vv):
    rows, width = ko_ref.shape
    kk[:WINDOW] = rim_ref[:, :width]
    kk[WINDOW:] = ko_ref[...]
    vv[:, :WINDOW] = rim_ref[:, width:].astype(F32).T.astype(BF16)
    vv[:, WINDOW:] = vo_ref[...].astype(F32).T.astype(BF16)
    bias = jnp.where(base_ref[0] > 0, 0.0, FAR).astype(F32)
    key_at, query_at = iota((HEAD, HEAD), 0), iota((HEAD, HEAD), 1)
    tiles = WINDOW // HEAD
    scale = 1.0 / math.sqrt(HEAD)
    for h in range(query_ref.shape[0]):
        for j in range(rows // HEAD):
            near = slice(j * HEAD, (j + tiles + 1) * HEAD)
            scores = dot(kk[near], query_ref[h, :, j * HEAD : (j + 1) * HEAD])
            pieces = []
            for t in range(tiles + 1):
                piece = scores[t * HEAD : (t + 1) * HEAD]
                if t == 0:
                    piece = jnp.where(key_at > query_at, piece, FAR)
                if t == tiles:
                    piece = jnp.where(key_at <= query_at, piece, FAR)
                if j + t < tiles:
                    piece = piece + bias
                pieces.append(piece)
            scores = jnp.concatenate(pieces, 0)
            peak = jnp.max(scores, axis=0, keepdims=True)
            grown = jnp.exp((scores - peak) * scale)
            share = 1.0 / jnp.sum(grown, axis=0, keepdims=True)
            mixed_vals = dot(vv[:, near], (grown * share).astype(BF16))
            out_ref[j * HEAD : (j + 1) * HEAD, head_cols(h)] = mixed_vals.T.astype(BF16)


def solve_kernel(heads, parts, first, digit_ref, base_ref, ridge_ref, *refs):
    part_refs, refs = refs[:parts], refs[parts:]
    q_ref, k_ref, v_ref, gain_ref, after_ref, out_ref, *refs = refs
    kk, kt, vt, kst, vst, coef, rates, causal, solved, state, res, way, rights, inners = refs
    prepare(heads, first, base_ref, ridge_ref, q_ref, k_ref, v_ref, kk, kt, res, vt, kst, vst, coef, rates, causal)
    chebyshev(
        heads, first, digit_ref, ridge_ref, part_refs,
        kk, kt, kst, coef, causal, solved, state, res, way, rights, inners,
    )
    mix(heads, first, digit_ref, part_refs, solved, kk, rates, vt, vst, gain_ref, out_ref)


def project_kernel(pairs, count, *refs):
    out_ref, last = refs[-1], refs[-2][...] if len(refs) > count + 1 else None
    for left, right, row in pairs:
        part = dot(refs[left][...], refs[right][row : row + refs[left].shape[1]])
        last = part if last is None else last + part
    out_ref[...] = last.astype(out_ref.dtype)


SMEM = pl.BlockSpec(memory_space=pltpu.SMEM)
VMEM = pl.BlockSpec(memory_space=pltpu.VMEM)


def call(kernel, outs, args, scalars=0, scratch=(), flops=0, nbytes=0):
    return pl.pallas_call(
        kernel,
        out_shape=outs,
        in_specs=[SMEM] * scalars + [VMEM] * (len(args) - scalars),
        out_specs=jax.tree.map(lambda _: VMEM, outs),
        scratch_shapes=list(scratch),
        compiler_params=pltpu.CompilerParams(vmem_limit_bytes=28 * 1024 * 1024),
        cost_estimate=pl.CostEstimate(flops=flops, bytes_accessed=nbytes, transcendentals=0),
    )(*args)


def rounds_of(count, stride):
    rounds = []
    while stride < count:
        left = count // stride
        radix = 4 if left % 4 == 0 else 2 if left % 2 == 0 else left
        rounds.append((stride, radix))
        stride *= radix
    return rounds


def partner(i, stride, radix, k):
    digit = (i // stride) % radix
    other = digit ^ k if radix in (2, 4) else (digit + k) % radix
    return i + (other - digit) * stride


def swap(x, axis, stride, radix, k):
    n = lax.axis_size(axis)
    return lax.ppermute(x, axis, [(i, partner(i, stride, radix, k)) for i in range(n)])


def source_digit(mine, stride, radix, k):
    digit = (mine // stride) % radix
    return digit ^ k if radix in (2, 4) else (digit - k) % radix


def before_flags(axis, first):
    mine = lax.axis_index(axis)
    flags = [mine < 0]
    for stride, radix in rounds_of(lax.axis_size(axis), first):
        digit = (mine // stride) % radix
        flags += [source_digit(mine, stride, radix, k) < digit for k in range(1, radix)]
    return jnp.stack(flags[1:] or flags).astype(jnp.int32)


def shards(
    mixer_queries, mixer_keys, mixer_values, window_keys, window_values, out_gain, ridge, out_weight
):
    rows = mixer_queries.shape[0]
    heads = ridge.shape[0]
    chunks = rows // CHUNK
    seq, head = lax.axis_size("seq"), lax.axis_size("head")
    base = (lax.axis_index("seq") * rows).astype(jnp.int32).reshape(1)
    shares = next(n for n in (4, 2, 1) if heads % n == 0 and seq % n == 0)
    own = heads // shares
    digit = (lax.axis_index("seq") % shares).astype(jnp.int32).reshape(1)
    flags = before_flags("seq", shares)
    sizes = group_sizes(heads)
    shape = jax.ShapeDtypeStruct
    width = window_keys.shape[1]
    block = shape((own, BOTH, HEAD), F32)

    def traded(parts):
        return [parts[0]] + [swap(parts[k], "seq", 1, shares, k) for k in range(1, shares)]

    rim = jnp.concatenate([window_keys, window_values], 1)[rows - WINDOW :]
    moments = call(
        functools.partial(moments_kernel, shares),
        (block,) * shares,
        (digit, mixer_keys, mixer_values),
        scalars=1,
    )
    moments = traded(moments)
    total = functools.reduce(jnp.add, moments)
    mine = lax.axis_index("head")
    cols = out_weight.shape[1] // head
    def columns(x, block, count=1):
        return lax.dynamic_slice_in_dim(x, block * cols, count * cols, 1)

    w_far = rim
    if head == 4:
        core = mine % 2
        near = swap(columns(out_weight, mine ^ 1), "head", 1, 4, 1)
        w_far = swap(columns(out_weight, (mine // 2 ^ 1) * 2, 2), "head", 1, 4, 2)
        relayed = swap(columns(w_far, core ^ 1), "head", 1, 4, 1)
        rights = [columns(out_weight, mine), near, columns(w_far, core), relayed]
    else:
        rights = [columns(out_weight, mine)]
        rights += [swap(columns(out_weight, partner(mine, 1, head, k)), "head", 1, head, k) for k in range(1, head)]
    common = jnp.zeros_like(total)
    rounds = rounds_of(seq, shares)
    i = 0
    for at, (stride, radix) in enumerate(rounds):
        got = [swap(total, "seq", stride, radix, k) for k in range(1, radix)]
        for part in got:
            common = common + jnp.where(flags[i] > 0, part, 0.0)
            i += 1
        if at + 1 < len(rounds):
            total = functools.reduce(jnp.add, got, total)
    priors = []
    for k in range(shares):
        prior = common
        for j in range(shares):
            if j != k:
                prior = prior + jnp.where((digit[0] ^ j) < (digit[0] ^ k), moments[j], 0.0)
        priors.append(prior)
    priors = traded(priors)
    rim = lax.ppermute(rim, "seq", [(i, (i + 1) % seq) for i in range(seq)])

    lefts = []
    attended, far = rim, w_far
    first = 0
    for per in sizes:
        (queries,) = call(
            functools.partial(solve_kernel, per, shares, first),
            (shape((per, HEAD, rows), BF16),),
            (
                digit, base, ridge, *priors, mixer_queries, mixer_keys, mixer_values,
                out_gain.reshape(1, -1), attended if first else out_gain.reshape(1, -1),
            ),
            scalars=3,
            scratch=(
                pltpu.VMEM((per, chunks, CHUNK, 2 * HEAD), BF16),
                pltpu.VMEM((per, chunks, HEAD, 2 * CHUNK), BF16),
                pltpu.VMEM((per, HEAD, rows), BF16),
                pltpu.VMEM((per, chunks - 1, HEAD, HEAD), F32),
                pltpu.VMEM((per, chunks - 1, HEAD, HEAD), F32),
                pltpu.VMEM((per, 2 * ITERS, rows), F32),
                pltpu.VMEM((per, rows, HEAD), F32),
                pltpu.VMEM((per, chunks, 3, HEAD, HEAD), F32),
                pltpu.VMEM((per, HEAD, rows), F32),
                *cheb_scratch(per, chunks),
            ),
            flops=10**10,
            nbytes=3 * 10**7,
        )
        (attended,) = call(
            attend_kernel,
            (shape((rows, per * HEAD), BF16),),
            (base, queries, rim, window_keys, window_values, far),
            scalars=1,
            scratch=(pltpu.VMEM((WINDOW + rows, width), BF16), pltpu.VMEM((width, WINDOW + rows), BF16)),
            flops=4 * 10**9,
            nbytes=15 * 10**6,
        )
        first += per
        if head == 4:
            far = swap(attended, "head", 1, 4, 2)
            lefts += [attended, swap(attended, "head", 1, 4, 1), far, swap(far, "head", 1, 4, 1)]
        else:
            lefts += [attended] + [swap(attended, "head", 1, head, k) for k in range(1, head)]
    def project(chosen, kind, *more):
        left = [lefts[g * head + k] for g, k in chosen]
        rows_of = [sum(sizes[:g]) * HEAD for g, _ in chosen]
        right = [rights[k] for _, k in chosen]
        count = 2 * len(chosen)
        pairs = [(i, len(chosen) + i, row) for i, row in enumerate(rows_of)]
        return call(
            functools.partial(project_kernel, pairs, count),
            (shape((rows, cols), kind),),
            (*left, *right, *more),
        )[0]

    last = len(sizes) - 1
    early = [(g, k) for g in range(len(sizes)) for k in range(head) if g < last or k < 2]
    late = [(last, k) for k in range(2, head)]
    if not late:
        return project(early, BF16)
    return project(late, BF16, project(early, F32))


def solution(mesh):
    return jax.shard_map(
        shards,
        mesh=mesh,
        in_specs=(
            P("seq", "head"),
            P("seq", "head"),
            P("seq", "head"),
            P("seq", "head"),
            P("seq", "head"),
            P("head"),
            P("head"),
            P("head", None),
        ),
        out_specs=P("seq", "head"),
        check_vma=False,
    )
```
